256 devices in a mesh: segment: 8 (over x, z_lo), expert: 32 (over y, z_hi, core).
Axes of the slice: x: 4, y: 4, z: 8 (z_hi: 4, z_lo: 2; z = z_hi * 2 + z_lo), core: 2. Of those that a mesh axis runs over, the one named last changes fastest.
Arguments:
- fwd_prev: bfloat16 [8, 2048, 1536], P('segment', 'expert'), may hold values from -6 to 6
- bwd_prev: bfloat16 [8, 2048, 1536], P('segment', 'expert'), may hold values from -6 to 6
- stored_in: bfloat16 [8, 2048, 1536], P('segment', 'expert'), may hold values from -6 to 6
- fwd_routes: int32 [8, 2048, 4], P('segment', 'expert'), may hold values from 0 to 31, all different within a row; in each aligned block of 64 rows (0 to 63, 64 to 127, ..., all dimensions but the last counted through in order) at most 16 rows name the same one
- fwd_gates: float32 [8, 2048, 4], P('segment', 'expert'), may hold values from 0.05 to 1
- bwd_routes: int32 [8, 2048, 4], P('segment', 'expert'), may hold values from 0 to 31, all different within a row; in each aligned block of 64 rows (0 to 63, 64 to 127, ..., all dimensions but the last counted through in order) at most 16 rows name the same one
- bwd_gates: float32 [8, 2048, 4], P('segment', 'expert'), may hold values from 0.05 to 1
- norm_gain: float32 [8, 1536], P('segment'), may hold values from 0.1 to 1.9
- w_up: bfloat16 [8, 32, 1536, 1536], P('segment', 'expert'), may hold values from -0.15625 to 0.15625
- w_down: bfloat16 [8, 32, 1536, 1536], P('segment', 'expert'), may hold values from -0.15625 to 0.15625
Outputs:
- fwd_out: bfloat16 [8, 2048, 1536], P('segment', 'expert')
- bwd_out: bfloat16 [8, 2048, 1536], P('segment', 'expert')
The draws below stay inside these ranges and needn't reach their ends.
Inputs may be any that keep to these rules, and one draw needn't show every extreme that they name: `fwd_routes`: the 4 ids of a token differ. In each aligned block of 64 tokens of a segment (the tokens of one device), no expert is named by more than 16 tokens, a bound that some block reaches. `bwd_routes`: the 4 ids of a token differ. In each aligned block of 64 tokens of a segment (the tokens of one device), no expert is named by more than 16 tokens, a bound that some block reaches.
All inputs are finite; a program needn't handle non-finite values.
Results may differ from the reference program's by a relative error of at most 0.0048.
Values may be sent and summed in bfloat16 or wider, within the bound.
A program may use at most 64 MiB of HBM per device.

```python
import math
import jax
import jax.numpy as jnp
import numpy as np
from jax import lax

D = 1536
FF = 1536
TOP = 4
TOK_DEV = 64
MOST = 16
EXPERTS = 32
TOKENS = 2048
N_SEGMENT = 8


def block_levels(rng, extent, pieces, low, high):
    level, own = 1.0, jax.random.fold_in(rng, 6)
    for dim, parts in pieces:
        draws = jnp.exp(jax.random.uniform(jax.random.fold_in(own, dim), (parts,), jnp.float32, low / len(pieces), high / len(pieces)))
        level = level * jnp.repeat(draws, extent[dim] // parts).reshape([-1 if axis == dim else 1 for axis in range(len(extent))])
    return level


def deal_out(own_key, own, number, rows, count, top, limit, slope):
    ranking = jax.random.permutation(own_key, count)
    packed, usual = shares(count, rows * top, limit, slope, True), shares(count, rows * top, limit, slope, False)
    places = jnp.arange(count)

    def named(lengths, rotation):
        used = int((lengths > 0).sum())
        fixed = max(1, used // 4)
        shifted = fixed + (places - fixed + rotation * (used - fixed)) % max(1, count - fixed)
        return jnp.zeros((count,), jnp.int32).at[ranking[jnp.where(places < fixed, places, shifted)]].set(jnp.asarray(lengths, jnp.int32))

    lengths = jnp.where(number % 4 == 0, named(packed, number // 4), named(usual, number - number // 4 - 1))
    mixed = jax.random.permutation(jax.random.fold_in(own, 3), count)
    donor, taker = mixed[0:count // 2 * 2:2], mixed[1:count // 2 * 2:2]
    margin = jnp.minimum(lengths[donor] - 1, limit - lengths[taker]) // 2
    margin = jnp.where((donor == ranking[0]) | (taker == ranking[0]) | (lengths[taker] == 0), 0, jnp.maximum(margin, 0))
    shifted = jax.random.randint(jax.random.fold_in(own, 4), (count // 2,), 0, 1 << 20) % (margin + 1)
    lengths = lengths.at[donor].add(-shifted).at[taker].add(shifted)
    items = jnp.searchsorted(jnp.cumsum(lengths), jnp.arange(rows * top), side="right").astype(jnp.int32)
    grid = items.reshape(top, rows).T
    grid = grid[jax.random.permutation(jax.random.fold_in(own, 1), rows)]
    rotation = jax.random.randint(jax.random.fold_in(own, 2), (rows, 1), 0, top)
    return jnp.take_along_axis(grid, (jnp.arange(top)[None, :] + rotation) % top, axis=1)


def shares(number_of, total, limit, slope, full):
    portions = [(1 << 20) // math.isqrt(standing ** slope) + 1 for standing in range(1, number_of + 1)]
    largest = limit if full else min(limit, max(-(-total // number_of), total * portions[0] // sum(portions)))
    least = 1 if total - largest >= number_of - 1 else 0
    holding, surplus = [largest] + [least] * (number_of - 1), total - largest - least * (number_of - 1)
    while surplus > 0:
        candidates = [i for i in range(1, number_of) if holding[i] < largest] or [i for i in range(1, number_of) if holding[i] < limit]
        mass, left = sum([portions[i] for i in candidates]), surplus
        for i in candidates:
            extra = min(limit - holding[i], max(1, left * portions[i] // mass), surplus)
            holding[i] = holding[i] + extra
            surplus = surplus - extra
    return np.array(holding)


def centred(own_key, dims, spread, reach, cuts=(), kind=jnp.bfloat16):
    result = jax.random.normal(own_key, dims, jnp.float32) * spread
    if len(cuts) > 0:
        result = block_levels(own_key, dims, cuts, -0.22, 0.18) * result
    return jnp.clip(result, min=-reach, max=reach).astype(kind)


def setup_inputs(seed: int = 0) -> dict:
    key_of = jax.random.split(jax.random.key(seed), 11)
    fwd_prev = centred(key_of[0], (N_SEGMENT, TOKENS, D), 1.0, 6.0, ((0, 8), (1, 32)))
    bwd_prev = centred(key_of[1], (N_SEGMENT, TOKENS, D), 1.0, 6.0, ((0, 8), (1, 32)))
    stored_in = centred(key_of[2], (N_SEGMENT, TOKENS, D), 1.0, 6.0, ((0, 8), (1, 32)))
    fwd_routes_keys = jax.random.split(jax.random.fold_in(key_of[3], 1), N_SEGMENT * TOKENS // TOK_DEV)
    fwd_routes_turns = jax.random.permutation(jax.random.fold_in(key_of[3], 3), N_SEGMENT * TOKENS // TOK_DEV)
    fwd_routes = jax.vmap(lambda own, number: deal_out(jax.random.fold_in(key_of[3], 2), own, number, TOK_DEV, EXPERTS, TOP, MOST, 2))(fwd_routes_keys, fwd_routes_turns).reshape((N_SEGMENT, TOKENS, TOP))
    fwd_gates = jnp.clip(jnp.exp(math.log(1.0) - 2.9957323 * jax.random.uniform(key_of[4], (N_SEGMENT, TOKENS, TOP), jnp.float32) ** block_levels(key_of[4], (N_SEGMENT, TOKENS, TOP), ((0, 8), (1, 32)), -0.2, 0.2)), 0.05, 1.0)
    bwd_routes_keys = jax.random.split(jax.random.fold_in(key_of[5], 1), N_SEGMENT * TOKENS // TOK_DEV)
    bwd_routes_turns = jax.random.permutation(jax.random.fold_in(key_of[5], 3), N_SEGMENT * TOKENS // TOK_DEV)
    bwd_routes = jax.vmap(lambda own, number: deal_out(jax.random.fold_in(key_of[5], 2), own, number, TOK_DEV, EXPERTS, TOP, MOST, 2))(bwd_routes_keys, bwd_routes_turns).reshape((N_SEGMENT, TOKENS, TOP))
    bwd_gates = jnp.clip(jnp.exp(math.log(1.0) - 2.9957323 * jax.random.uniform(key_of[6], (N_SEGMENT, TOKENS, TOP), jnp.float32) ** block_levels(key_of[6], (N_SEGMENT, TOKENS, TOP), ((0, 8), (1, 32)), -0.2, 0.2)), 0.05, 1.0)
    norm_gain = jnp.clip(1.0 + 0.18 * jax.random.normal(key_of[7], (N_SEGMENT, D), jnp.float32), 0.1, 1.9)
    w_up = centred(key_of[8], (N_SEGMENT, EXPERTS, D, FF), D ** -0.5, 0.15625, ((0, 8), (1, 32)))
    w_down = centred(key_of[9], (N_SEGMENT, EXPERTS, FF, D), FF ** -0.5, 0.15625, ((0, 8), (1, 32)))
    return {"fwd_prev": fwd_prev, "bwd_prev": bwd_prev, "stored_in": stored_in, "fwd_routes": fwd_routes, "fwd_gates": fwd_gates, "bwd_routes": bwd_routes, "bwd_gates": bwd_gates, "norm_gain": norm_gain, "w_up": w_up, "w_down": w_down}


norm_eps = 1e-05

def normalize(rows, gain):
    values = rows.astype(jnp.float32)
    scale = lax.rsqrt(lax.optimization_barrier(jnp.mean(values * values, axis=-1, keepdims=True)) + norm_eps)
    return (values, scale, (values * scale * gain).astype(jnp.bfloat16))

def expert_forward(rows, up_weight, down_weight):
    pre = jnp.dot(rows, up_weight, preferred_element_type=jnp.float32)
    act = jax.nn.silu(pre).astype(jnp.bfloat16)
    return jnp.dot(act, down_weight, preferred_element_type=jnp.float32).astype(jnp.bfloat16)

def expert_backward(rows, cotan, up_weight, down_weight):
    pre = jnp.dot(rows, up_weight, preferred_element_type=jnp.float32)
    sigma = jax.nn.sigmoid(pre)
    deriv = sigma * (1.0 + pre * (1.0 - sigma))
    back = lax.dot_general(cotan, down_weight, (((1,), (1,)), ((), ())), preferred_element_type=jnp.float32)
    inner = (back * deriv).astype(jnp.bfloat16)
    return lax.dot_general(inner, up_weight, (((1,), (1,)), ((), ())), preferred_element_type=jnp.float32).astype(jnp.bfloat16)

def placement_of(routes):
    flat = routes.reshape(-1).astype(jnp.int32)
    onehot = (flat[:, None] == jnp.arange(EXPERTS, dtype=jnp.int32)[None, :]).astype(jnp.int32)
    rank = lax.optimization_barrier(jnp.sum((jnp.cumsum(onehot, axis=0) - onehot) * onehot, axis=1))
    return (flat * (EXPERTS * MOST) + rank).astype(jnp.int32)

def dispatch(rows, dest):
    buffer = jnp.zeros((EXPERTS * EXPERTS * MOST, rows.shape[1]), rows.dtype)
    buffer = buffer.at[dest].set(jnp.repeat(rows, TOP, axis=0))
    return buffer.reshape(EXPERTS, EXPERTS * MOST, rows.shape[1])

def one_segment(items):
    arriving, cotangent, stored, f_routes, f_gates, b_routes, b_gates, gain, up_all, down_all = items
    f_values, f_scale, f_normed = normalize(arriving, gain)
    b_values, b_scale, b_normed = normalize(stored, gain)
    f_dest = placement_of(f_routes)
    b_dest = placement_of(b_routes)
    f_buf = dispatch(f_normed, f_dest)
    b_buf = dispatch(b_normed, b_dest)
    c_buf = dispatch(cotangent, b_dest)

    def serve(group):
        rows_f, rows_b, rows_c, up_weight, down_weight = group
        return (expert_forward(rows_f, up_weight, down_weight), expert_backward(rows_b, rows_c, up_weight, down_weight))
    f_res, b_res = lax.map(serve, (f_buf, b_buf, c_buf, up_all, down_all))
    f_rows = f_res.reshape(-1, D)[f_dest].reshape(TOKENS, TOP, D).astype(jnp.float32)
    b_rows = b_res.reshape(-1, D)[b_dest].reshape(TOKENS, TOP, D).astype(jnp.float32)
    fwd_out = (f_values + lax.optimization_barrier(jnp.sum(f_gates[:, :, None] * f_rows, axis=1))).astype(jnp.bfloat16)
    weighted = gain * lax.optimization_barrier(jnp.sum(b_gates[:, :, None] * b_rows, axis=1))
    correction = b_values * b_scale ** 3 * lax.optimization_barrier(jnp.mean(b_values * weighted, axis=-1, keepdims=True))
    bwd_out = (cotangent.astype(jnp.float32) + b_scale * weighted - correction).astype(jnp.bfloat16)
    return (fwd_out, bwd_out)

def reference(fwd_prev, bwd_prev, stored_in, fwd_routes, fwd_gates, bwd_routes, bwd_gates, norm_gain, w_up, w_down):
    arriving = jnp.roll(fwd_prev, 1, axis=0)
    cotangent = jnp.roll(bwd_prev, -1, axis=0)
    fwd_out, bwd_out = lax.map(one_segment, (arriving, cotangent, stored_in, fwd_routes, fwd_gates, bwd_routes, bwd_gates, norm_gain, w_up, w_down))
    return (fwd_out, bwd_out)
```

```python
import functools

import jax
import jax.numpy as jnp
from jax import lax
from jax.experimental import pallas as pl
from jax.experimental.pallas import tpu as pltpu
from jax.sharding import PartitionSpec as P

MESH = pl.DeviceIdType.MESH
TOK = 64
D = 1536
MOST = 16
SLOTS = 128
ROWS = 512
HALF = D // 2
TILE = 256
EPS = 1e-05

B, C, F = 0, 1, 2
OB_, OF_ = 0, 1
H0, H1 = (0, HALF), (HALF, HALF)
FULL = (0, D)


def kernel(
    fwd_ref,
    bwd_ref,
    stored_ref,
    meta_ref,
    gain_ref,
    up_hbm,
    down_hbm,
    fout_ref,
    bout_ref,
    up,
    down,
    meta,
    ag,
    fraw,
    sb,
    rx,
    mid,
    ob,
    rt,
    ps,
    fr,
    hs,
    acc,
    pt,
    ghi,
    glo,
    wsem,
    meta_s,
    meta_r,
    seg_s,
    ag_s,
    ag_r,
    y_s,
    rx_r,
    ret_s,
    rt_r,
    fr_s,
    fr_r,
    hs_s,
    hs_r,
):
    s = lax.axis_index("segment")
    e = lax.axis_index("expert")
    y, z, c = e // 8, (e // 2) % 4, e % 2
    g = 2 * (s % 2) - 1

    def at(dy, role, core, ds=0):
        return (
            (s + ds + 8) % 8,
            ((y + dy) % 4) * 8 + ((z + role * g + 4) % 4) * 2 + core,
        )

    def remote(src, dst, ssem, rsem, device):
        copy = pltpu.make_async_remote_copy(
            src_ref=src, dst_ref=dst, send_sem=ssem, recv_sem=rsem, device_id=device, device_id_type=MESH
        )
        copy.start()

    def wait(ref, sem):
        pltpu.make_async_copy(ref, ref, sem).wait()

    up_copy = pltpu.make_async_copy(up_hbm, up, wsem.at[0])
    down_copy = pltpu.make_async_copy(down_hbm, down, wsem.at[1])
    up_copy.start()
    down_copy.start()

    partners = [at(dy, 0, core) for dy in (1, 2, 3) for core in (0, 1)]
    partners += [at(0, 0, 1 - c), at(0, 1, c), at(0, -1, c), at(0, 2, c)]
    partners += [at(0, 0, c, 1), at(0, 1, c, 1), at(0, 0, c, -1), at(0, 1, c, -1)]
    barrier = pltpu.get_barrier_semaphore()
    for device in partners:
        pl.semaphore_signal(barrier, inc=1, device_id=device, device_id_type=MESH)

    gain = gain_ref[...]

    def scale_of(values):
        return lax.rsqrt(jnp.mean(values * values, axis=-1, keepdims=True) + EPS)

    def normalized(rows):
        values = rows.astype(jnp.float32)
        return (values * scale_of(values) * gain).astype(jnp.bfloat16)

    slot = lax.broadcasted_iota(jnp.int32, (SLOTS, SLOTS), 0)
    group = slot // MOST
    expert_of = (((y + group // 2) % 4) * 8 + z * 2 + group % 2).astype(jnp.float32)
    rank_of = (slot % MOST).astype(jnp.float32)
    before = (slot < lax.broadcasted_iota(jnp.int32, (SLOTS, SLOTS), 1)).astype(jnp.bfloat16)

    def places(which, role, gates):
        base = 8 * which
        chosen = jnp.zeros((SLOTS, SLOTS), jnp.float32)
        weight = jnp.zeros((SLOTS, SLOTS), jnp.float32)
        for k in range(4):
            same = (meta[role, base + k : base + k + 1, :] == expert_of).astype(jnp.float32)
            chosen += same
            if gates:
                weight += same * meta[role, base + 4 + k : base + 5 + k, :]
        rank = jnp.dot(chosen.astype(jnp.bfloat16), before, preferred_element_type=jnp.float32)
        placed = chosen * (rank == rank_of).astype(jnp.float32)
        return placed, weight

    def make_pack(which, role):
        placed, _ = places(which, role, False)
        pt[which, role] = placed.astype(jnp.bfloat16)

    def make_gates(which, role):
        placed, weight = places(which, role, True)
        gates = jnp.transpose(placed * weight)[:TOK]
        high = gates.astype(jnp.bfloat16)
        ghi[which, role] = high
        glo[which, role] = (gates - high.astype(jnp.float32)).astype(jnp.bfloat16)

    def pack(a, role, cols):
        which = 0 if a < F else 1
        sb[a, role * SLOTS : (role + 1) * SLOTS, pl.ds(*cols)] = jnp.dot(
            pt[which, role][:, :TOK], ag[a, role, :, pl.ds(*cols)], preferred_element_type=jnp.float32
        ).astype(jnp.bfloat16)

    def spread(src, dst, role, cols, ssem, rsem):
        def rows(k):
            return pl.ds(pl.multiple_of((role * 8 + k) * MOST, MOST), MOST)

        for dy in (2, 1, 3):
            for core in (0, 1):
                remote(
                    src.at[rows(dy * 2 + core), pl.ds(*cols)],
                    dst.at[rows((4 - dy) * 2 + c), pl.ds(*cols)],
                    ssem,
                    rsem,
                    at(dy, 0, core),
                )
        remote(src.at[rows(1 - c), pl.ds(*cols)], dst.at[rows(c), pl.ds(*cols)], ssem, rsem, at(0, 0, 1 - c))
        pltpu.make_async_copy(src.at[rows(c), pl.ds(*cols)], dst.at[rows(c), pl.ds(*cols)], rsem).start()

    def dispatch(a, role, cols):
        spread(sb.at[a], rx.at[a], role, cols, y_s.at[a], rx_r.at[a])

    def give_back(o, role, cols, part):
        spread(ob.at[o], rt.at[o], role, cols, ret_s.at[o], rt_r.at[o, role, part])

    meta[0] = meta_ref[...]
    ag[B, 0] = normalized(stored_ref[...])
    make_pack(0, 0)
    pack(B, 0, FULL)

    pl.semaphore_wait(barrier, len(partners))

    for i, role in enumerate((1, 3, 2)):
        remote(meta.at[0], meta.at[4 - role], meta_s.at[i], meta_r.at[4 - role], at(0, role, c))
    near, other = at(0, 1, c), at(0, -1, c)

    def half(ref, h):
        return ref.at[:, pl.ds(h * HALF, HALF)]

    for i, (role, h) in enumerate(((1, 0), (3, 1), (1, 1), (3, 0))):
        dest = near if role == 1 else other
        remote(half(ag.at[B, 0], h), half(ag.at[B, 4 - role], h), ag_s.at[B, i], ag_r.at[B, 4 - role, h], dest)
    dispatch(B, 0, FULL)

    for role in (3, 1, 2):
        wait(meta.at[role], meta_r.at[role])
        make_pack(0, role)

    def hop_b(role, h):
        wait(half(ag.at[B, role], h), ag_r.at[B, role, h])
        if (role, h) == (3, 0):
            remote(half(ag.at[B, 3], 0), half(ag.at[B, 2], 0), ag_s.at[B, 4], ag_r.at[B, 2, 0], near)
        if (role, h) == (1, 1):
            remote(half(ag.at[B, 1], 1), half(ag.at[B, 2], 1), ag_s.at[B, 5], ag_r.at[B, 2, 1], other)
        pack(B, role, (h * HALF, HALF))
        dispatch(B, role, (h * HALF, HALF))

    hop_b(3, 0)
    hop_b(1, 1)
    remote(bwd_ref, ag.at[C, 0], seg_s.at[0], ag_r.at[C, 0, 0], at(0, 0, c, -1))
    remote(bwd_ref, ag.at[C, 1], seg_s.at[1], ag_r.at[C, 1, 0], at(0, 1, c, -1))
    hop_b(3, 1)
    hop_b(1, 0)

    def hop(a, role):
        blocks = ag.at[C] if a == C else fraw
        wait(blocks.at[role], ag_r.at[a, role, 0])
        if role == 0:
            remote(blocks.at[0], blocks.at[3], ag_s.at[a, 0], ag_r.at[a, 3, 0], near)
        if role == 1:
            remote(blocks.at[1], blocks.at[2], ag_s.at[a, 1], ag_r.at[a, 2, 0], other)
        if a == F:
            ag[F, role] = normalized(fraw[role])
        pack(a, role, FULL)
        dispatch(a, role, FULL)

    for role in range(4):
        make_pack(1, role)
    hop(C, 0)
    hop(C, 1)
    hop_b(2, 0)
    hop_b(2, 1)
    remote(fwd_ref, fraw.at[0], seg_s.at[2], ag_r.at[F, 0, 0], at(0, 0, c, 1))
    remote(fwd_ref, fraw.at[1], seg_s.at[3], ag_r.at[F, 1, 0], at(0, 1, c, 1))
    for role in range(4):
        make_gates(0, role)
        make_gates(1, role)
    hop(C, 3)
    hop(C, 2)
    hop(F, 0)
    hop(F, 1)

    up_copy.wait()
    down_copy.wait()
    wait(rx.at[B], rx_r.at[B])
    wait(rx.at[C], rx_r.at[C])

    def tile(n):
        return pl.ds(pl.multiple_of(n * TILE, TILE), TILE)

    nt = (((1,), (1,)), ((), ()))

    def back_in(n, carry):
        pre = jnp.dot(rx[B], up[:, tile(n)], preferred_element_type=jnp.float32)
        sigma = jax.nn.sigmoid(pre)
        deriv = sigma * (1.0 + pre * (1.0 - sigma))
        back = lax.dot_general(rx[C], down[tile(n), :], nt, preferred_element_type=jnp.float32)
        mid[:, tile(n)] = (back * deriv).astype(jnp.bfloat16)
        return carry

    def back_out(n, carry):
        ob[OB_, :, tile(n)] = lax.dot_general(
            mid[...], up[tile(n), :], nt, preferred_element_type=jnp.float32
        ).astype(jnp.bfloat16)
        return carry

    def front_in(n, carry):
        pre = jnp.dot(rx[F], up[:, tile(n)], preferred_element_type=jnp.float32)
        mid[:, tile(n)] = jax.nn.silu(pre).astype(jnp.bfloat16)
        return carry

    def front_out(n, carry):
        ob[OF_, :, tile(n)] = jnp.dot(mid[...], down[:, tile(n)], preferred_element_type=jnp.float32).astype(
            jnp.bfloat16
        )
        return carry

    lax.fori_loop(0, 3, back_in, 0)
    hop(F, 3)
    lax.fori_loop(3, 6, back_in, 0)
    hop(F, 2)
    lax.fori_loop(0, 6, back_out, 0)

    give_back(OB_, 2, H0, 0)
    give_back(OB_, 2, H1, 1)
    give_back(OB_, 1, H0, 0)
    give_back(OB_, 3, H0, 0)
    give_back(OB_, 1, H1, 1)
    give_back(OB_, 3, H1, 1)
    give_back(OB_, 0, H0, 0)
    give_back(OB_, 0, H1, 1)

    wait(rx.at[F], rx_r.at[F])
    lax.fori_loop(0, 6, front_in, 0)
    lax.fori_loop(0, 6, front_out, 0)

    def gather(o, role, h):
        lane = pl.ds(h * HALF, HALF)
        block = rt.at[o, pl.ds(role * SLOTS, SLOTS), lane]
        wait(block, rt_r.at[o, role, h])
        rows = block[...]
        total = jnp.dot(ghi[o, role], rows, preferred_element_type=jnp.float32) + jnp.dot(
            glo[o, role], rows, preferred_element_type=jnp.float32
        )
        if role == 0:
            acc[o, :, lane] = total
            return
        if (role, h) in ((1, 0), (3, 1)):
            wait(half(fr.at[o], h), fr_r.at[o, h])
            total += fr[o, :, lane].astype(jnp.float32)
        ps[o, role, :, lane] = total.astype(jnp.bfloat16)
        if role == 2:
            remote(half(ps.at[o, 2], h), half(fr.at[o], h), fr_s.at[o, h], fr_r.at[o, h], near if h == 0 else other)
        else:
            i = 0 if role == 1 else 1
            remote(
                half(ps.at[o, role], h),
                half(hs.at[o, i], h),
                hs_s.at[o, i, h],
                hs_r.at[o, i, h],
                near if role == 1 else other,
            )

    def summed(o, h):
        lane = pl.ds(h * HALF, HALF)
        for i in (0, 1):
            wait(half(hs.at[o, i], h), hs_r.at[o, i, h])
        return acc[o, :, lane] + hs[o, 0, :, lane].astype(jnp.float32) + hs[o, 1, :, lane].astype(jnp.float32)

    gather(OB_, 2, 0)
    gather(OB_, 2, 1)
    give_back(OF_, 2, H0, 0)
    give_back(OF_, 2, H1, 1)
    gather(OB_, 1, 0)
    gather(OB_, 3, 0)
    give_back(OF_, 1, H0, 0)
    give_back(OF_, 3, H0, 0)
    gather(OB_, 1, 1)
    gather(OB_, 3, 1)
    give_back(OF_, 1, H1, 1)
    give_back(OF_, 3, H1, 1)
    gather(OB_, 0, 0)
    gather(OB_, 0, 1)
    give_back(OF_, 0, H0, 0)
    give_back(OF_, 0, H1, 1)
    gather(OF_, 2, 0)
    gather(OF_, 2, 1)

    for h in (0, 1):
        acc[OB_, :, pl.ds(h * HALF, HALF)] = summed(OB_, h)
    weighted = gain * acc[OB_]
    values = stored_ref[...].astype(jnp.float32)
    scale = scale_of(values)
    correction = values * (scale * scale * scale) * jnp.mean(values * weighted, axis=-1, keepdims=True)
    bout_ref[...] = (ag[C, 0].astype(jnp.float32) + scale * weighted - correction).astype(jnp.bfloat16)

    gather(OF_, 1, 0)
    gather(OF_, 3, 0)
    gather(OF_, 1, 1)
    gather(OF_, 3, 1)
    gather(OF_, 0, 0)
    gather(OF_, 0, 1)
    for h in (0, 1):
        lane = pl.ds(h * HALF, HALF)
        fout_ref[:, lane] = (fraw[0, :, lane].astype(jnp.float32) + summed(OF_, h)).astype(jnp.bfloat16)

    for i in range(3):
        wait(meta.at[0], meta_s.at[i])
    for i in range(4):
        wait(fraw.at[0], seg_s.at[i])
    for i in range(6):
        wait(half(ag.at[B, 0], 0), ag_s.at[B, i])
    for a in (C, F):
        for i in range(2):
            wait(ag.at[a, 0], ag_s.at[a, i])
    sent = pl.ds(0, ROWS * 7 // 8)
    for a in (B, C, F):
        wait(sb.at[a, sent], y_s.at[a])
    for o in (OB_, OF_):
        wait(ob.at[o, sent], ret_s.at[o])
        for h in (0, 1):
            wait(half(fr.at[o], h), fr_s.at[o, h])
            for i in (0, 1):
                wait(half(hs.at[o, i], h), hs_s.at[o, i, h])


def section(fwd_prev, bwd_prev, stored_in, fwd_routes, fwd_gates, bwd_routes, bwd_gates, norm_gain, w_up, w_down):
    lines = jnp.concatenate(
        [bwd_routes[0].astype(jnp.float32), bwd_gates[0], fwd_routes[0].astype(jnp.float32), fwd_gates[0]], axis=1
    ).T
    lines = jnp.pad(lines, ((0, 0), (0, SLOTS - TOK)), constant_values=-1.0)
    vmem = pl.BlockSpec(memory_space=pltpu.VMEM)
    anywhere = pl.BlockSpec(memory_space=pl.ANY)
    bf16, f32 = jnp.bfloat16, jnp.float32
    dma = pltpu.SemaphoreType.DMA
    out = jax.ShapeDtypeStruct((TOK, D), bf16)
    fwd_out, bwd_out = pl.pallas_call(
        kernel,
        out_shape=(out, out),
        in_specs=[vmem] * 5 + [anywhere] * 2,
        out_specs=(vmem, vmem),
        scratch_shapes=[
            pltpu.VMEM((D, D), bf16),
            pltpu.VMEM((D, D), bf16),
            pltpu.VMEM((4, 16, SLOTS), f32),
            pltpu.VMEM((3, 4, TOK, D), bf16),
            pltpu.VMEM((4, TOK, D), bf16),
            pltpu.VMEM((3, ROWS, D), bf16),
            pltpu.VMEM((3, ROWS, D), bf16),
            pltpu.VMEM((ROWS, D), bf16),
            pltpu.VMEM((2, ROWS, D), bf16),
            pltpu.VMEM((2, ROWS, D), bf16),
            pltpu.VMEM((2, 4, TOK, D), bf16),
            pltpu.VMEM((2, TOK, D), bf16),
            pltpu.VMEM((2, 2, TOK, D), bf16),
            pltpu.VMEM((2, TOK, D), f32),
            pltpu.VMEM((2, 4, SLOTS, SLOTS), bf16),
            pltpu.VMEM((2, 4, TOK, SLOTS), bf16),
            pltpu.VMEM((2, 4, TOK, SLOTS), bf16),
            dma((2,)),
            dma((3,)),
            dma((4,)),
            dma((4,)),
            dma((3, 6)),
            dma((3, 4, 2)),
            dma((3,)),
            dma((3,)),
            dma((2,)),
            dma((2, 4, 2)),
            dma((2, 2)),
            dma((2, 2)),
            dma((2, 2, 2)),
            dma((2, 2, 2)),
        ],
        compiler_params=pltpu.CompilerParams(collective_id=0, has_side_effects=True, vmem_limit_bytes=56 * 2**20),
        cost_estimate=pl.CostEstimate(
            flops=5 * 2 * ROWS * D * D, bytes_accessed=2 * D * D * 2 + 5 * TOK * D * 2, transcendentals=2 * ROWS * D
        ),
        name="section",
    )(fwd_prev[0], bwd_prev[0], stored_in[0], lines, norm_gain, w_up[0, 0], w_down[0, 0])
    return fwd_out[None], bwd_out[None]


def solution(mesh):
    block = P("segment", "expert", None)
    weight = P("segment", "expert", None, None)
    return jax.shard_map(
        section,
        mesh=mesh,
        in_specs=(block,) * 7 + (P("segment", None), weight, weight),
        out_specs=(block, block),
        check_vma=False,
    )
```

```python
import functools

import jax
import jax.numpy as jnp
from jax import lax
from jax.experimental import pallas as pl
from jax.experimental.pallas import tpu as pltpu
from jax.sharding import PartitionSpec as P

MESH = pl.DeviceIdType.MESH
TOK = 64
D = 1536
MOST = 16
SLOTS = 128
ROWS = 512
HALF = D // 2
TILE = 256
EPS = 1e-05

B, C, F = 0, 1, 2
OB_, OF_ = 0, 1
H0, H1 = (0, HALF), (HALF, HALF)
FULL = (0, D)


def kernel(
    fwd_ref,
    bwd_ref,
    stored_hbm,
    b_routes_hbm,
    b_gates_hbm,
    f_routes_hbm,
    f_gates_hbm,
    gain_hbm,
    up_hbm,
    down_hbm,
    fout_ref,
    bout_ref,
    up,
    down,
    stored_ref,
    b_routes_ref,
    b_gates_ref,
    f_routes_ref,
    f_gates_ref,
    gain_ref,
    meta,
    ag,
    fraw,
    sb,
    rx,
    mid,
    ob,
    rt,
    ps,
    fr,
    hs,
    acc,
    pt,
    ghi,
    glo,
    load_sem,
    wsem,
    meta_s,
    meta_r,
    seg_s,
    ag_s,
    ag_r,
    y_s,
    rx_r,
    ret_s,
    rt_r,
    fr_s,
    fr_r,
    hs_s,
    hs_r,
):
    s = lax.axis_index("segment")
    e = lax.axis_index("expert")
    y, z, c = e // 8, (e // 2) % 4, e % 2
    g = 2 * (s % 2) - 1

    def at(dy, role, core, ds=0):
        return (
            (s + ds + 8) % 8,
            ((y + dy) % 4) * 8 + ((z + role * g + 4) % 4) * 2 + core,
        )

    def remote(src, dst, ssem, rsem, device):
        copy = pltpu.make_async_remote_copy(
            src_ref=src, dst_ref=dst, send_sem=ssem, recv_sem=rsem, device_id=device, device_id_type=MESH
        )
        copy.start()

    def wait(ref, sem):
        pltpu.make_async_copy(ref, ref, sem).wait()

    partners = [at(dy, 0, core) for dy in (1, 2, 3) for core in (0, 1)]
    partners += [at(0, 0, 1 - c), at(0, 1, c), at(0, -1, c), at(0, 2, c)]
    partners += [at(0, 0, c, 1), at(0, 1, c, 1), at(0, 0, c, -1), at(0, 1, c, -1)]
    barrier = pltpu.get_barrier_semaphore()
    for device in partners:
        pl.semaphore_signal(barrier, inc=1, device_id=device, device_id_type=MESH)

    loads = [
        pltpu.make_async_copy(src, dst, load_sem.at[i])
        for i, (src, dst) in enumerate(
            (
                (stored_hbm, stored_ref),
                (b_routes_hbm, b_routes_ref),
                (b_gates_hbm, b_gates_ref),
                (f_routes_hbm, f_routes_ref),
                (f_gates_hbm, f_gates_ref),
                (gain_hbm, gain_ref),
            )
        )
    ]
    for load in loads:
        load.start()
    up_copy = pltpu.make_async_copy(up_hbm, up, wsem.at[0])
    down_copy = pltpu.make_async_copy(down_hbm, down, wsem.at[1])
    up_copy.start()
    down_copy.start()

    def scale_of(values):
        return lax.rsqrt(jnp.mean(values * values, axis=-1, keepdims=True) + EPS)

    def normalized(rows):
        values = rows.astype(jnp.float32)
        return (values * scale_of(values) * gain_ref[...]).astype(jnp.bfloat16)

    slot = lax.broadcasted_iota(jnp.int32, (SLOTS, SLOTS), 0)
    group = slot // MOST
    expert_of = (((y + group // 2) % 4) * 8 + z * 2 + group % 2).astype(jnp.float32)
    rank_of = (slot % MOST).astype(jnp.float32)
    before = (slot < lax.broadcasted_iota(jnp.int32, (SLOTS, SLOTS), 1)).astype(jnp.bfloat16)

    def places(which, role, gates):
        base = 8 * which
        chosen = jnp.zeros((SLOTS, SLOTS), jnp.float32)
        weight = jnp.zeros((SLOTS, SLOTS), jnp.float32)
        for k in range(4):
            same = (meta[role, base + k : base + k + 1, :] == expert_of).astype(jnp.float32)
            chosen += same
            if gates:
                weight += same * meta[role, base + 4 + k : base + 5 + k, :]
        rank = jnp.dot(chosen.astype(jnp.bfloat16), before, preferred_element_type=jnp.float32)
        placed = chosen * (rank == rank_of).astype(jnp.float32)
        return placed, weight

    def make_pack(which, role):
        placed, _ = places(which, role, False)
        pt[which, role] = placed.astype(jnp.bfloat16)

    def make_gates(which, role):
        placed, weight = places(which, role, True)
        gates = jnp.transpose(placed * weight)[:TOK]
        high = gates.astype(jnp.bfloat16)
        ghi[which, role] = high
        glo[which, role] = (gates - high.astype(jnp.float32)).astype(jnp.bfloat16)

    def pack(a, role, cols):
        which = 0 if a < F else 1
        sb[a, role * SLOTS : (role + 1) * SLOTS, pl.ds(*cols)] = jnp.dot(
            pt[which, role][:, :TOK], ag[a, role, :, pl.ds(*cols)], preferred_element_type=jnp.float32
        ).astype(jnp.bfloat16)

    def spread(src, dst, role, cols, ssem, rsem):
        def rows(k):
            return pl.ds(pl.multiple_of((role * 8 + k) * MOST, MOST), MOST)

        for dy in (2, 1, 3):
            for core in (0, 1):
                remote(
                    src.at[rows(dy * 2 + core), pl.ds(*cols)],
                    dst.at[rows((4 - dy) * 2 + c), pl.ds(*cols)],
                    ssem,
                    rsem,
                    at(dy, 0, core),
                )
        remote(src.at[rows(1 - c), pl.ds(*cols)], dst.at[rows(c), pl.ds(*cols)], ssem, rsem, at(0, 0, 1 - c))
        pltpu.make_async_copy(src.at[rows(c), pl.ds(*cols)], dst.at[rows(c), pl.ds(*cols)], rsem).start()

    def dispatch(a, role, cols):
        spread(sb.at[a], rx.at[a], role, cols, y_s.at[a], rx_r.at[a])

    def give_back(o, role, cols, part):
        spread(ob.at[o], rt.at[o], role, cols, ret_s.at[o], rt_r.at[o, role, part])

    near, other = at(0, 1, c), at(0, -1, c)

    def half(ref, h):
        return ref.at[:, pl.ds(h * HALF, HALF)]

    def send_c(h):
        for role in (0, 1):
            remote(
                half(bwd_ref, h), half(ag.at[C, role], h), seg_s.at[2 * h + role], ag_r.at[C, role, h], at(0, role, c, -1)
            )

    pl.semaphore_wait(barrier, len(partners))
    send_c(0)
    for load in loads:
        load.wait()
    meta[0] = jnp.full((16, SLOTS), -1.0, jnp.float32)
    for i, ref in enumerate((b_routes_ref, b_gates_ref, f_routes_ref, f_gates_ref)):
        meta[0, 4 * i : 4 * i + 4, :TOK] = ref[...].astype(jnp.float32)
    for i, role in enumerate((1, 3, 2)):
        remote(meta.at[0], meta.at[4 - role], meta_s.at[i], meta_r.at[4 - role], at(0, role, c))
    send_c(1)
    ag[B, 0] = normalized(stored_ref[...])
    make_pack(0, 0)
    pack(B, 0, FULL)
    dispatch(B, 0, FULL)
    for i, (role, h) in enumerate(((1, 0), (3, 1), (1, 1), (3, 0))):
        dest = near if role == 1 else other
        remote(half(ag.at[B, 0], h), half(ag.at[B, 4 - role], h), ag_s.at[B, i], ag_r.at[B, 4 - role, h], dest)


    def hop_b(role, h):
        wait(half(ag.at[B, role], h), ag_r.at[B, role, h])
        if (role, h) == (3, 0):
            remote(half(ag.at[B, 3], 0), half(ag.at[B, 2], 0), ag_s.at[B, 4], ag_r.at[B, 2, 0], near)
        if (role, h) == (1, 1):
            remote(half(ag.at[B, 1], 1), half(ag.at[B, 2], 1), ag_s.at[B, 5], ag_r.at[B, 2, 1], other)
        pack(B, role, (h * HALF, HALF))
        dispatch(B, role, (h * HALF, HALF))

    def hop_c(role, h):
        wait(half(ag.at[C, role], h), ag_r.at[C, role, h])
        if role == 0:
            remote(half(ag.at[C, 0], h), half(ag.at[C, 3], h), ag_s.at[C, h], ag_r.at[C, 3, h], near)
        if role == 1:
            remote(half(ag.at[C, 1], h), half(ag.at[C, 2], h), ag_s.at[C, 2 + h], ag_r.at[C, 2, h], other)
        pack(C, role, (h * HALF, HALF))
        dispatch(C, role, (h * HALF, HALF))

    def hop_f(role):
        wait(fraw.at[role], ag_r.at[F, role, 0])
        if role == 0:
            remote(fraw.at[0], fraw.at[3], ag_s.at[F, 0], ag_r.at[F, 3, 0], near)
        if role == 1:
            remote(fraw.at[1], fraw.at[2], ag_s.at[F, 1], ag_r.at[F, 2, 0], other)
        ag[F, role] = normalized(fraw[role])
        pack(F, role, FULL)
        dispatch(F, role, FULL)

    hop_c(0, 0)
    for role in (1, 3, 2):
        wait(meta.at[role], meta_r.at[role])
        make_pack(0, role)
    hop_c(1, 0)
    hop_c(0, 1)
    hop_c(1, 1)
    hop_b(3, 0)
    hop_b(1, 1)
    for role in (0, 1):
        remote(fwd_ref, fraw.at[role], seg_s.at[4 + role], ag_r.at[F, role, 0], at(0, role, c, 1))
    hop_b(3, 1)
    hop_b(1, 0)
    for role in range(4):
        make_pack(1, role)
    hop_c(3, 0)
    hop_c(2, 0)
    hop_c(3, 1)
    hop_c(2, 1)
    hop_b(2, 0)
    hop_b(2, 1)
    for role in range(4):
        make_gates(0, role)
        make_gates(1, role)
    hop_f(0)
    hop_f(1)

    up_copy.wait()
    down_copy.wait()
    wait(rx.at[B], rx_r.at[B])
    wait(rx.at[C], rx_r.at[C])

    def tile(n):
        return pl.ds(pl.multiple_of(n * TILE, TILE), TILE)

    nt = (((1,), (1,)), ((), ()))

    def back_in(n, carry):
        pre = jnp.dot(rx[B], up[:, tile(n)], preferred_element_type=jnp.float32)
        sigma = jax.nn.sigmoid(pre)
        deriv = sigma * (1.0 + pre * (1.0 - sigma))
        back = lax.dot_general(rx[C], down[tile(n), :], nt, preferred_element_type=jnp.float32)
        mid[:, tile(n)] = (back * deriv).astype(jnp.bfloat16)
        return carry

    def back_out(n, carry):
        ob[OB_, :, tile(n)] = lax.dot_general(
            mid[...], up[tile(n), :], nt, preferred_element_type=jnp.float32
        ).astype(jnp.bfloat16)
        return carry

    def front_in(n, carry):
        pre = jnp.dot(rx[F], up[:, tile(n)], preferred_element_type=jnp.float32)
        mid[:, tile(n)] = jax.nn.silu(pre).astype(jnp.bfloat16)
        return carry

    def front_out(n, carry):
        ob[OF_, :, tile(n)] = jnp.dot(mid[...], down[:, tile(n)], preferred_element_type=jnp.float32).astype(
            jnp.bfloat16
        )
        return carry

    lax.fori_loop(0, 3, back_in, 0)
    hop_f(3)
    hop_f(2)
    lax.fori_loop(3, 6, back_in, 0)
    lax.fori_loop(0, 6, back_out, 0)

    give_back(OB_, 2, H0, 0)
    give_back(OB_, 2, H1, 1)
    give_back(OB_, 1, H0, 0)
    give_back(OB_, 3, H0, 0)
    give_back(OB_, 1, H1, 1)
    give_back(OB_, 3, H1, 1)

    wait(rx.at[F], rx_r.at[F])
    lax.fori_loop(0, 6, front_in, 0)
    lax.fori_loop(0, 6, front_out, 0)

    def gather(o, role, h):
        lane = pl.ds(h * HALF, HALF)
        block = rt.at[o, pl.ds(role * SLOTS, SLOTS), lane]
        wait(block, rt_r.at[o, role, h])
        rows = block[...]
        total = jnp.dot(ghi[o, role], rows, preferred_element_type=jnp.float32) + jnp.dot(
            glo[o, role], rows, preferred_element_type=jnp.float32
        )
        if role == 0:
            acc[o, :, lane] = total
            return
        if (role, h) in ((1, 0), (3, 1)):
            wait(half(fr.at[o], h), fr_r.at[o, h])
            total += fr[o, :, lane].astype(jnp.float32)
        ps[o, role, :, lane] = total.astype(jnp.bfloat16)
        if role == 2:
            remote(half(ps.at[o, 2], h), half(fr.at[o], h), fr_s.at[o, h], fr_r.at[o, h], near if h == 0 else other)
        else:
            i = 0 if role == 1 else 1
            remote(
                half(ps.at[o, role], h),
                half(hs.at[o, i], h),
                hs_s.at[o, i, h],
                hs_r.at[o, i, h],
                near if role == 1 else other,
            )

    def summed(o, h):
        lane = pl.ds(h * HALF, HALF)
        for i in (0, 1):
            wait(half(hs.at[o, i], h), hs_r.at[o, i, h])
        return acc[o, :, lane] + hs[o, 0, :, lane].astype(jnp.float32) + hs[o, 1, :, lane].astype(jnp.float32)

    gather(OB_, 2, 0)
    gather(OB_, 2, 1)
    for part, cols in enumerate((H0, H1)):
        give_back(OF_, 2, cols, part)
    gather(OB_, 1, 0)
    gather(OB_, 3, 0)
    give_back(OF_, 1, H0, 0)
    give_back(OF_, 3, H0, 0)
    gather(OB_, 1, 1)
    gather(OB_, 3, 1)
    give_back(OF_, 1, H1, 1)
    give_back(OF_, 3, H1, 1)
    for o in (OB_, OF_):
        for part, cols in enumerate((H0, H1)):
            give_back(o, 0, cols, part)
    gather(OF_, 2, 0)
    gather(OF_, 2, 1)
    gather(OF_, 1, 0)
    gather(OF_, 3, 0)
    gather(OF_, 1, 1)
    gather(OF_, 3, 1)
    gather(OB_, 0, 0)
    gather(OB_, 0, 1)
    for h in (0, 1):
        acc[OB_, :, pl.ds(h * HALF, HALF)] = summed(OB_, h)
    weighted = gain_ref[...] * acc[OB_]
    values = stored_ref[...].astype(jnp.float32)
    scale = scale_of(values)
    correction = values * (scale * scale * scale) * jnp.mean(values * weighted, axis=-1, keepdims=True)
    bout_ref[...] = (ag[C, 0].astype(jnp.float32) + scale * weighted - correction).astype(jnp.bfloat16)

    for h in (0, 1):
        gather(OF_, 0, h)
        lane = pl.ds(h * HALF, HALF)
        fout_ref[:, lane] = (fraw[0, :, lane].astype(jnp.float32) + summed(OF_, h)).astype(jnp.bfloat16)

    for i in range(3):
        wait(meta.at[0], meta_s.at[i])
    for i in range(4):
        wait(half(ag.at[C, 0], 0), seg_s.at[i])
        wait(half(ag.at[C, 0], 0), ag_s.at[C, i])
    for i in range(6):
        wait(half(ag.at[B, 0], 0), ag_s.at[B, i])
    for i in range(2):
        wait(fraw.at[0], seg_s.at[4 + i])
        wait(fraw.at[0], ag_s.at[F, i])
    sent = pl.ds(0, ROWS * 7 // 8)
    for a in (B, C, F):
        wait(sb.at[a, sent], y_s.at[a])
    for o in (OB_, OF_):
        wait(ob.at[o, sent], ret_s.at[o])
        for h in (0, 1):
            wait(half(fr.at[o], h), fr_s.at[o, h])
            for i in (0, 1):
                wait(half(hs.at[o, i], h), hs_s.at[o, i, h])


def finish(fwd_ref, bwd_ref, fout_ref, bout_ref, sem):
    first = pltpu.make_async_copy(fwd_ref, fout_ref, sem.at[0])
    second = pltpu.make_async_copy(bwd_ref, bout_ref, sem.at[1])
    first.start()
    second.start()
    first.wait()
    second.wait()


def section(fwd_prev, bwd_prev, stored_in, fwd_routes, fwd_gates, bwd_routes, bwd_gates, norm_gain, w_up, w_down):
    vmem = pl.BlockSpec(memory_space=pltpu.VMEM)
    anywhere = pl.BlockSpec(memory_space=pl.ANY)
    bf16, f32 = jnp.bfloat16, jnp.float32
    dma = pltpu.SemaphoreType.DMA
    out = jax.ShapeDtypeStruct((TOK, D), bf16)
    kept = pltpu.VMEM((TOK, D), bf16)
    fwd_out, bwd_out = pl.pallas_call(
        kernel,
        out_shape=(kept, kept),
        in_specs=[anywhere] * 10,
        out_specs=(vmem, vmem),
        scratch_shapes=[
            pltpu.VMEM((D, D), bf16),
            pltpu.VMEM((D, D), bf16),
            pltpu.VMEM((TOK, D), bf16),
            pltpu.VMEM((4, TOK), jnp.int32),
            pltpu.VMEM((4, TOK), f32),
            pltpu.VMEM((4, TOK), jnp.int32),
            pltpu.VMEM((4, TOK), f32),
            pltpu.VMEM((1, D), f32),
            pltpu.VMEM((4, 16, SLOTS), f32),
            pltpu.VMEM((3, 4, TOK, D), bf16),
            pltpu.VMEM((4, TOK, D), bf16),
            pltpu.VMEM((3, ROWS, D), bf16),
            pltpu.VMEM((3, ROWS, D), bf16),
            pltpu.VMEM((ROWS, D), bf16),
            pltpu.VMEM((2, ROWS, D), bf16),
            pltpu.VMEM((2, ROWS, D), bf16),
            pltpu.VMEM((2, 4, TOK, D), bf16),
            pltpu.VMEM((2, TOK, D), bf16),
            pltpu.VMEM((2, 2, TOK, D), bf16),
            pltpu.VMEM((2, TOK, D), f32),
            pltpu.VMEM((2, 4, SLOTS, SLOTS), bf16),
            pltpu.VMEM((2, 4, TOK, SLOTS), bf16),
            pltpu.VMEM((2, 4, TOK, SLOTS), bf16),
            dma((6,)),
            dma((2,)),
            dma((3,)),
            dma((4,)),
            dma((6,)),
            dma((3, 6)),
            dma((3, 4, 2)),
            dma((3,)),
            dma((3,)),
            dma((2,)),
            dma((2, 4, 2)),
            dma((2, 2)),
            dma((2, 2)),
            dma((2, 2, 2)),
            dma((2, 2, 2)),
        ],
        compiler_params=pltpu.CompilerParams(collective_id=0, has_side_effects=True, vmem_limit_bytes=56 * 2**20),
        cost_estimate=pl.CostEstimate(
            flops=5 * 2 * ROWS * D * D, bytes_accessed=2 * D * D * 2 + 5 * TOK * D * 2, transcendentals=2 * ROWS * D
        ),
        name="section",
    )(
        fwd_prev[0],
        bwd_prev[0],
        stored_in[0],
        bwd_routes[0].T,
        bwd_gates[0].T,
        fwd_routes[0].T,
        fwd_gates[0].T,
        norm_gain,
        w_up[0, 0],
        w_down[0, 0],
    )
    fwd_out, bwd_out = pl.pallas_call(
        finish,
        out_shape=(out, out),
        in_specs=[vmem] * 2,
        out_specs=(anywhere, anywhere),
        scratch_shapes=[dma((2,))],
        name="finish",
    )(*(pltpu.with_memory_space_constraint(v, pltpu.VMEM) for v in (fwd_out, bwd_out)))
    return fwd_out[None], bwd_out[None]


def solution(mesh):
    block = P("segment", "expert", None)
    weight = P("segment", "expert", None, None)
    return jax.shard_map(
        section,
        mesh=mesh,
        in_specs=(block,) * 7 + (P("segment", None), weight, weight),
        out_specs=(block, block),
        check_vma=False,
    )
```

```python
import functools

import jax
import jax.numpy as jnp
from jax import lax
from jax.experimental import pallas as pl
from jax.experimental.pallas import tpu as pltpu
from jax.sharding import PartitionSpec as P

MESH = pl.DeviceIdType.MESH
TOK = 64
D = 1536
MOST = 16
SLOTS = 128
ROWS = 512
HALF = D // 2
TILE = 256
EPS = 1e-05

B, C, F = 0, 1, 2
OB_, OF_ = 0, 1
H0, H1 = (0, HALF), (HALF, HALF)
FULL = (0, D)


def kernel(
    fwd_ref,
    bwd_ref,
    stored_hbm,
    b_routes_hbm,
    b_gates_hbm,
    f_routes_hbm,
    f_gates_hbm,
    gain_hbm,
    up_hbm,
    down_hbm,
    fout_ref,
    bout_ref,
    up,
    down,
    stored_ref,
    b_routes_ref,
    b_gates_ref,
    f_routes_ref,
    f_gates_ref,
    gain_ref,
    meta,
    ag,
    fraw,
    sb,
    rx,
    mid,
    ob,
    rt,
    ps,
    fr,
    hs,
    acc,
    pt,
    ghi,
    glo,
    load_sem,
    wsem,
    meta_s,
    meta_r,
    seg_s,
    ag_s,
    ag_r,
    y_s,
    rx_r,
    ret_s,
    rt_r,
    fr_s,
    fr_r,
    hs_s,
    hs_r,
):
    s = lax.axis_index("segment")
    e = lax.axis_index("expert")
    y, z, c = e // 8, (e // 2) % 4, e % 2
    g = 2 * (s % 2) - 1

    def at(dy, role, core, ds=0):
        return (
            (s + ds + 8) % 8,
            ((y + dy) % 4) * 8 + ((z + role * g + 4) % 4) * 2 + core,
        )

    def remote(src, dst, ssem, rsem, device):
        copy = pltpu.make_async_remote_copy(
            src_ref=src, dst_ref=dst, send_sem=ssem, recv_sem=rsem, device_id=device, device_id_type=MESH
        )
        copy.start()

    def wait(ref, sem):
        pltpu.make_async_copy(ref, ref, sem).wait()

    partners = [at(dy, 0, core) for dy in (1, 2, 3) for core in (0, 1)]
    partners += [at(0, 0, 1 - c), at(0, 1, c), at(0, -1, c), at(0, 2, c)]
    partners += [at(0, 0, c, 1), at(0, 1, c, 1), at(0, 0, c, -1), at(0, 1, c, -1)]
    barrier = pltpu.get_barrier_semaphore()
    for device in partners:
        pl.semaphore_signal(barrier, inc=1, device_id=device, device_id_type=MESH)

    loads = [
        pltpu.make_async_copy(src, dst, load_sem.at[i])
        for i, (src, dst) in enumerate(
            (
                (stored_hbm, stored_ref),
                (b_routes_hbm, b_routes_ref),
                (b_gates_hbm, b_gates_ref),
                (f_routes_hbm, f_routes_ref),
                (f_gates_hbm, f_gates_ref),
                (gain_hbm, gain_ref),
            )
        )
    ]
    for load in loads:
        load.start()
    up_copy = pltpu.make_async_copy(up_hbm, up, wsem.at[0])
    down_copy = pltpu.make_async_copy(down_hbm, down, wsem.at[1])
    up_copy.start()
    down_copy.start()

    def scale_of(values):
        return lax.rsqrt(jnp.mean(values * values, axis=-1, keepdims=True) + EPS)

    def normalized(rows):
        values = rows.astype(jnp.float32)
        return (values * scale_of(values) * gain_ref[...]).astype(jnp.bfloat16)

    slot = lax.broadcasted_iota(jnp.int32, (SLOTS, SLOTS), 0)
    group = slot // MOST
    expert_of = (((y + group // 2) % 4) * 8 + z * 2 + group % 2).astype(jnp.float32)
    rank_of = (slot % MOST).astype(jnp.float32)
    before = (slot < lax.broadcasted_iota(jnp.int32, (SLOTS, SLOTS), 1)).astype(jnp.bfloat16)

    def places(which, role, gates):
        base = 8 * which
        chosen = jnp.zeros((SLOTS, SLOTS), jnp.float32)
        weight = jnp.zeros((SLOTS, SLOTS), jnp.float32)
        for k in range(4):
            same = (meta[role, base + k : base + k + 1, :] == expert_of).astype(jnp.float32)
            chosen += same
            if gates:
                weight += same * meta[role, base + 4 + k : base + 5 + k, :]
        rank = jnp.dot(chosen.astype(jnp.bfloat16), before, preferred_element_type=jnp.float32)
        placed = chosen * (rank == rank_of).astype(jnp.float32)
        return placed, weight

    def make_pack(which, role):
        placed, _ = places(which, role, False)
        pt[which, role] = placed.astype(jnp.bfloat16)

    def make_gates(which, role):
        placed, weight = places(which, role, True)
        gates = jnp.transpose(placed * weight)[:TOK]
        high = gates.astype(jnp.bfloat16)
        ghi[which, role] = high
        glo[which, role] = (gates - high.astype(jnp.float32)).astype(jnp.bfloat16)

    def pack(a, role, cols):
        which = 0 if a < F else 1
        sb[a, role * SLOTS : (role + 1) * SLOTS, pl.ds(*cols)] = jnp.dot(
            pt[which, role][:, :TOK], ag[a, role, :, pl.ds(*cols)], preferred_element_type=jnp.float32
        ).astype(jnp.bfloat16)

    def spread(src, dst, role, cols, ssem, rsem):
        def rows(k):
            return pl.ds(pl.multiple_of((role * 8 + k) * MOST, MOST), MOST)

        for dy in (2, 1, 3):
            for core in (0, 1):
                remote(
                    src.at[rows(dy * 2 + core), pl.ds(*cols)],
                    dst.at[rows((4 - dy) * 2 + c), pl.ds(*cols)],
                    ssem,
                    rsem,
                    at(dy, 0, core),
                )
        remote(src.at[rows(1 - c), pl.ds(*cols)], dst.at[rows(c), pl.ds(*cols)], ssem, rsem, at(0, 0, 1 - c))
        pltpu.make_async_copy(src.at[rows(c), pl.ds(*cols)], dst.at[rows(c), pl.ds(*cols)], rsem).start()

    def dispatch(a, role, cols):
        spread(sb.at[a], rx.at[a], role, cols, y_s.at[a], rx_r.at[a])

    def give_back(o, role, cols, part):
        spread(ob.at[o], rt.at[o], role, cols, ret_s.at[o], rt_r.at[o, role, part])

    near, other = at(0, 1, c), at(0, -1, c)

    def half(ref, h):
        return ref.at[:, pl.ds(h * HALF, HALF)]

    def send_c(h):
        for role in (0, 1):
            remote(
                half(bwd_ref, h), half(ag.at[C, role], h), seg_s.at[2 * h + role], ag_r.at[C, role, h], at(0, role, c, -1)
            )

    pl.semaphore_wait(barrier, len(partners))
    send_c(0)
    for load in loads:
        load.wait()
    meta[0] = jnp.full((16, SLOTS), -1.0, jnp.float32)
    for i, ref in enumerate((b_routes_ref, b_gates_ref, f_routes_ref, f_gates_ref)):
        meta[0, 4 * i : 4 * i + 4, :TOK] = ref[...].astype(jnp.float32)
    for i, role in enumerate((1, 3, 2)):
        remote(meta.at[0], meta.at[4 - role], meta_s.at[i], meta_r.at[4 - role], at(0, role, c))
    send_c(1)
    for role in (0, 1):
        remote(fwd_ref, fraw.at[role], seg_s.at[4 + role], ag_r.at[F, role, 0], at(0, role, c, 1))
    ag[B, 0] = normalized(stored_ref[...])
    make_pack(0, 0)
    pack(B, 0, FULL)
    dispatch(B, 0, FULL)
    for i, (role, h) in enumerate(((1, 0), (3, 1), (1, 1), (3, 0))):
        dest = near if role == 1 else other
        remote(half(ag.at[B, 0], h), half(ag.at[B, 4 - role], h), ag_s.at[B, i], ag_r.at[B, 4 - role, h], dest)


    def hop_b(role, h):
        wait(half(ag.at[B, role], h), ag_r.at[B, role, h])
        if (role, h) == (3, 0):
            remote(half(ag.at[B, 3], 0), half(ag.at[B, 2], 0), ag_s.at[B, 4], ag_r.at[B, 2, 0], near)
        if (role, h) == (1, 1):
            remote(half(ag.at[B, 1], 1), half(ag.at[B, 2], 1), ag_s.at[B, 5], ag_r.at[B, 2, 1], other)
        pack(B, role, (h * HALF, HALF))
        dispatch(B, role, (h * HALF, HALF))

    def hop_c(role, h):
        wait(half(ag.at[C, role], h), ag_r.at[C, role, h])
        pack(C, role, (h * HALF, HALF))
        dispatch(C, role, (h * HALF, HALF))

    def hop_f(role):
        wait(fraw.at[role], ag_r.at[F, role, 0])
        if role == 0:
            remote(fraw.at[0], fraw.at[3], ag_s.at[F, 0], ag_r.at[F, 3, 0], near)
        if role == 1:
            remote(fraw.at[1], fraw.at[2], ag_s.at[F, 1], ag_r.at[F, 2, 0], other)
        ag[F, role] = normalized(fraw[role])
        pack(F, role, FULL)
        dispatch(F, role, FULL)

    hop_c(0, 0)
    for role in (1, 3, 2):
        wait(meta.at[role], meta_r.at[role])
        make_pack(0, role)
    hop_c(1, 0)
    hop_c(0, 1)
    hop_c(1, 1)
    make_pack(1, 0)
    make_pack(1, 1)
    hop_f(0)
    hop_f(1)
    for h in (0, 1):
        remote(half(ag.at[C, 0], h), half(ag.at[C, 3], h), ag_s.at[C, h], ag_r.at[C, 3, h], near)
        remote(half(ag.at[C, 1], h), half(ag.at[C, 2], h), ag_s.at[C, 2 + h], ag_r.at[C, 2, h], other)
    hop_b(3, 0)
    hop_b(1, 1)
    hop_b(3, 1)
    hop_b(1, 0)
    make_pack(1, 3)
    make_pack(1, 2)
    for role in range(4):
        make_gates(1, role)
        make_gates(0, role)
    hop_f(3)
    hop_f(2)
    hop_c(3, 0)
    hop_c(2, 0)
    hop_c(3, 1)
    hop_c(2, 1)
    hop_b(2, 0)
    hop_b(2, 1)


    def tile(n):
        return pl.ds(pl.multiple_of(n * TILE, TILE), TILE)

    nt = (((1,), (1,)), ((), ()))

    def back_in(n, carry):
        pre = jnp.dot(rx[B], up[:, tile(n)], preferred_element_type=jnp.float32)
        sigma = jax.nn.sigmoid(pre)
        deriv = sigma * (1.0 + pre * (1.0 - sigma))
        back = lax.dot_general(rx[C], down[tile(n), :], nt, preferred_element_type=jnp.float32)
        mid[:, tile(n)] = (back * deriv).astype(jnp.bfloat16)
        return carry

    def back_out(n, carry):
        ob[OB_, :, tile(n)] = lax.dot_general(
            mid[...], up[tile(n), :], nt, preferred_element_type=jnp.float32
        ).astype(jnp.bfloat16)
        return carry

    def front_in(n, carry):
        pre = jnp.dot(rx[F], up[:, tile(n)], preferred_element_type=jnp.float32)
        mid[:, tile(n)] = jax.nn.silu(pre).astype(jnp.bfloat16)
        return carry

    def front_out(n, carry):
        ob[OF_, :, tile(n)] = jnp.dot(mid[...], down[:, tile(n)], preferred_element_type=jnp.float32).astype(
            jnp.bfloat16
        )
        return carry

    def gather(o, role, h):
        lane = pl.ds(h * HALF, HALF)
        block = rt.at[o, pl.ds(role * SLOTS, SLOTS), lane]
        wait(block, rt_r.at[o, role, h])
        rows = block[...]
        total = jnp.dot(ghi[o, role], rows, preferred_element_type=jnp.float32) + jnp.dot(
            glo[o, role], rows, preferred_element_type=jnp.float32
        )
        if role == 0:
            acc[o, :, lane] = total
            return
        if (role, h) in ((1, 0), (3, 1)):
            wait(half(fr.at[o], h), fr_r.at[o, h])
            total += fr[o, :, lane].astype(jnp.float32)
        ps[o, role, :, lane] = total.astype(jnp.bfloat16)
        if role == 2:
            remote(half(ps.at[o, 2], h), half(fr.at[o], h), fr_s.at[o, h], fr_r.at[o, h], near if h == 0 else other)
        else:
            i = 0 if role == 1 else 1
            remote(
                half(ps.at[o, role], h),
                half(hs.at[o, i], h),
                hs_s.at[o, i, h],
                hs_r.at[o, i, h],
                near if role == 1 else other,
            )

    def summed(o, h):
        lane = pl.ds(h * HALF, HALF)
        for i in (0, 1):
            wait(half(hs.at[o, i], h), hs_r.at[o, i, h])
        return acc[o, :, lane] + hs[o, 0, :, lane].astype(jnp.float32) + hs[o, 1, :, lane].astype(jnp.float32)

    def give_back_sides(o):
        for part, cols in enumerate((H0, H1)):
            give_back(o, 1, cols, part)
            give_back(o, 3, cols, part)

    up_copy.wait()
    down_copy.wait()
    wait(rx.at[F], rx_r.at[F])
    lax.fori_loop(0, 6, front_in, 0)
    lax.fori_loop(0, 6, front_out, 0)
    give_back(OF_, 2, H0, 0)
    give_back(OF_, 2, H1, 1)
    give_back_sides(OF_)

    wait(rx.at[B], rx_r.at[B])
    wait(rx.at[C], rx_r.at[C])
    lax.fori_loop(0, 3, back_in, 0)
    gather(OF_, 2, 0)
    gather(OF_, 2, 1)
    lax.fori_loop(3, 6, back_in, 0)
    lax.fori_loop(0, 3, back_out, 0)
    give_back(OB_, 2, H0, 0)
    lax.fori_loop(3, 6, back_out, 0)
    give_back(OB_, 2, H1, 1)
    gather(OF_, 1, 0)
    gather(OF_, 3, 0)
    gather(OF_, 1, 1)
    gather(OF_, 3, 1)
    give_back_sides(OB_)
    gather(OB_, 2, 0)
    gather(OB_, 2, 1)
    for o in (OB_, OF_):
        for part, cols in enumerate((H0, H1)):
            give_back(o, 0, cols, part)
    gather(OB_, 1, 0)
    gather(OB_, 3, 0)
    gather(OB_, 1, 1)
    gather(OB_, 3, 1)
    gather(OB_, 0, 0)
    gather(OB_, 0, 1)
    for h in (0, 1):
        acc[OB_, :, pl.ds(h * HALF, HALF)] = summed(OB_, h)
    weighted = gain_ref[...] * acc[OB_]
    values = stored_ref[...].astype(jnp.float32)
    scale = scale_of(values)
    correction = values * (scale * scale * scale) * jnp.mean(values * weighted, axis=-1, keepdims=True)
    bout_ref[...] = (ag[C, 0].astype(jnp.float32) + scale * weighted - correction).astype(jnp.bfloat16)

    for h in (0, 1):
        gather(OF_, 0, h)
        lane = pl.ds(h * HALF, HALF)
        fout_ref[:, lane] = (fraw[0, :, lane].astype(jnp.float32) + summed(OF_, h)).astype(jnp.bfloat16)

    for i in range(3):
        wait(meta.at[0], meta_s.at[i])
    for i in range(4):
        wait(half(ag.at[C, 0], 0), seg_s.at[i])
        wait(half(ag.at[C, 0], 0), ag_s.at[C, i])
    for i in range(6):
        wait(half(ag.at[B, 0], 0), ag_s.at[B, i])
    for i in range(2):
        wait(fraw.at[0], seg_s.at[4 + i])
        wait(fraw.at[0], ag_s.at[F, i])
    sent = pl.ds(0, ROWS * 7 // 8)
    for a in (B, C, F):
        wait(sb.at[a, sent], y_s.at[a])
    for o in (OB_, OF_):
        wait(ob.at[o, sent], ret_s.at[o])
        for h in (0, 1):
            wait(half(fr.at[o], h), fr_s.at[o, h])
            for i in (0, 1):
                wait(half(hs.at[o, i], h), hs_s.at[o, i, h])


def finish(fwd_ref, bwd_ref, fout_ref, bout_ref, sem):
    first = pltpu.make_async_copy(fwd_ref, fout_ref, sem.at[0])
    second = pltpu.make_async_copy(bwd_ref, bout_ref, sem.at[1])
    first.start()
    second.start()
    first.wait()
    second.wait()


def section(fwd_prev, bwd_prev, stored_in, fwd_routes, fwd_gates, bwd_routes, bwd_gates, norm_gain, w_up, w_down):
    vmem = pl.BlockSpec(memory_space=pltpu.VMEM)
    anywhere = pl.BlockSpec(memory_space=pl.ANY)
    bf16, f32 = jnp.bfloat16, jnp.float32
    dma = pltpu.SemaphoreType.DMA
    out = jax.ShapeDtypeStruct((TOK, D), bf16)
    kept = pltpu.VMEM((TOK, D), bf16)
    fwd_out, bwd_out = pl.pallas_call(
        kernel,
        out_shape=(kept, kept),
        in_specs=[anywhere] * 10,
        out_specs=(vmem, vmem),
        scratch_shapes=[
            pltpu.VMEM((D, D), bf16),
            pltpu.VMEM((D, D), bf16),
            pltpu.VMEM((TOK, D), bf16),
            pltpu.VMEM((4, TOK), jnp.int32),
            pltpu.VMEM((4, TOK), f32),
            pltpu.VMEM((4, TOK), jnp.int32),
            pltpu.VMEM((4, TOK), f32),
            pltpu.VMEM((1, D), f32),
            pltpu.VMEM((4, 16, SLOTS), f32),
            pltpu.VMEM((3, 4, TOK, D), bf16),
            pltpu.VMEM((4, TOK, D), bf16),
            pltpu.VMEM((3, ROWS, D), bf16),
            pltpu.VMEM((3, ROWS, D), bf16),
            pltpu.VMEM((ROWS, D), bf16),
            pltpu.VMEM((2, ROWS, D), bf16),
            pltpu.VMEM((2, ROWS, D), bf16),
            pltpu.VMEM((2, 4, TOK, D), bf16),
            pltpu.VMEM((2, TOK, D), bf16),
            pltpu.VMEM((2, 2, TOK, D), bf16),
            pltpu.VMEM((2, TOK, D), f32),
            pltpu.VMEM((2, 4, SLOTS, SLOTS), bf16),
            pltpu.VMEM((2, 4, TOK, SLOTS), bf16),
            pltpu.VMEM((2, 4, TOK, SLOTS), bf16),
            dma((6,)),
            dma((2,)),
            dma((3,)),
            dma((4,)),
            dma((6,)),
            dma((3, 6)),
            dma((3, 4, 2)),
            dma((3,)),
            dma((3,)),
            dma((2,)),
            dma((2, 4, 2)),
            dma((2, 2)),
            dma((2, 2)),
            dma((2, 2, 2)),
            dma((2, 2, 2)),
        ],
        compiler_params=pltpu.CompilerParams(collective_id=0, has_side_effects=True, vmem_limit_bytes=56 * 2**20),
        cost_estimate=pl.CostEstimate(
            flops=5 * 2 * ROWS * D * D, bytes_accessed=2 * D * D * 2 + 5 * TOK * D * 2, transcendentals=2 * ROWS * D
        ),
        name="section",
    )(
        fwd_prev[0],
        bwd_prev[0],
        stored_in[0],
        bwd_routes[0].T,
        bwd_gates[0].T,
        fwd_routes[0].T,
        fwd_gates[0].T,
        norm_gain,
        w_up[0, 0],
        w_down[0, 0],
    )
    fwd_out, bwd_out = pl.pallas_call(
        finish,
        out_shape=(out, out),
        in_specs=[vmem] * 2,
        out_specs=(anywhere, anywhere),
        scratch_shapes=[dma((2,))],
        name="finish",
    )(*(pltpu.with_memory_space_constraint(v, pltpu.VMEM) for v in (fwd_out, bwd_out)))
    return fwd_out[None], bwd_out[None]


def solution(mesh):
    block = P("segment", "expert", None)
    weight = P("segment", "expert", None, None)
    return jax.shard_map(
        section,
        mesh=mesh,
        in_specs=(block,) * 7 + (P("segment", None), weight, weight),
        out_specs=(block, block),
        check_vma=False,
    )
```

```python
import functools

import jax
import jax.numpy as jnp
from jax import lax
from jax.experimental import pallas as pl
from jax.experimental.pallas import tpu as pltpu
from jax.sharding import PartitionSpec as P

MESH = pl.DeviceIdType.MESH
TOK = 64
D = 1536
MOST = 16
SLOTS = 128
ROWS = 512
HALF = D // 2
TILE = 256
EPS = 1e-05

B, C, F = 0, 1, 2
OB_, OF_ = 0, 1
H0, H1 = (0, HALF), (HALF, HALF)
FULL = (0, D)


def kernel(
    fwd_ref,
    bwd_ref,
    stored_hbm,
    b_routes_hbm,
    b_gates_hbm,
    f_routes_hbm,
    f_gates_hbm,
    gain_hbm,
    up_hbm,
    down_hbm,
    fout_ref,
    bout_ref,
    up,
    down,
    stored_ref,
    b_routes_ref,
    b_gates_ref,
    f_routes_ref,
    f_gates_ref,
    gain_ref,
    meta,
    ag,
    fraw,
    sb,
    rx,
    mid,
    ob,
    rt,
    ps,
    fr,
    hs,
    acc,
    pt,
    ghi,
    glo,
    load_sem,
    wsem,
    meta_s,
    meta_r,
    seg_s,
    ag_s,
    ag_r,
    y_s,
    rx_r,
    ret_s,
    rt_r,
    fr_s,
    fr_r,
    hs_s,
    hs_r,
):
    s = lax.axis_index("segment")
    e = lax.axis_index("expert")
    y, z, c = e // 8, (e // 2) % 4, e % 2
    g = 2 * (s % 2) - 1

    def at(dy, role, core, ds=0):
        return (
            (s + ds + 8) % 8,
            ((y + dy) % 4) * 8 + ((z + role * g + 4) % 4) * 2 + core,
        )

    def remote(src, dst, ssem, rsem, device):
        copy = pltpu.make_async_remote_copy(
            src_ref=src, dst_ref=dst, send_sem=ssem, recv_sem=rsem, device_id=device, device_id_type=MESH
        )
        copy.start()

    def wait(ref, sem):
        pltpu.make_async_copy(ref, ref, sem).wait()

    partners = [at(dy, 0, core) for dy in (1, 2, 3) for core in (0, 1)]
    partners += [at(0, 0, 1 - c), at(0, 1, c), at(0, -1, c), at(0, 2, c)]
    partners += [at(0, 0, c, 1), at(0, 1, c, 1), at(0, 0, c, -1), at(0, 1, c, -1)]
    barrier = pltpu.get_barrier_semaphore()
    for device in partners:
        pl.semaphore_signal(barrier, inc=1, device_id=device, device_id_type=MESH)

    loads = [
        pltpu.make_async_copy(src, dst, load_sem.at[i])
        for i, (src, dst) in enumerate(
            (
                (stored_hbm, stored_ref),
                (b_routes_hbm, b_routes_ref),
                (b_gates_hbm, b_gates_ref),
                (f_routes_hbm, f_routes_ref),
                (f_gates_hbm, f_gates_ref),
                (gain_hbm, gain_ref),
            )
        )
    ]
    for load in loads:
        load.start()
    up_copy = pltpu.make_async_copy(up_hbm, up, wsem.at[0])
    down_copy = pltpu.make_async_copy(down_hbm, down, wsem.at[1])
    up_copy.start()
    down_copy.start()

    def scale_of(values):
        return lax.rsqrt(jnp.mean(values * values, axis=-1, keepdims=True) + EPS)

    def normalized(rows):
        values = rows.astype(jnp.float32)
        return (values * scale_of(values) * gain_ref[...]).astype(jnp.bfloat16)

    slot = lax.broadcasted_iota(jnp.int32, (SLOTS, SLOTS), 0)
    group = slot // MOST
    expert_of = (((y + group // 2) % 4) * 8 + z * 2 + group % 2).astype(jnp.float32)
    rank_of = (slot % MOST).astype(jnp.float32)
    before = (slot < lax.broadcasted_iota(jnp.int32, (SLOTS, SLOTS), 1)).astype(jnp.bfloat16)

    def places(which, role, gates):
        base = 8 * which
        chosen = jnp.zeros((SLOTS, SLOTS), jnp.float32)
        weight = jnp.zeros((SLOTS, SLOTS), jnp.float32)
        for k in range(4):
            same = (meta[role, base + k : base + k + 1, :] == expert_of).astype(jnp.float32)
            chosen += same
            if gates:
                weight += same * meta[role, base + 4 + k : base + 5 + k, :]
        rank = jnp.dot(chosen.astype(jnp.bfloat16), before, preferred_element_type=jnp.float32)
        placed = chosen * (rank == rank_of).astype(jnp.float32)
        return placed, weight

    def make_pack(which, role):
        placed, _ = places(which, role, False)
        pt[which, role] = placed.astype(jnp.bfloat16)

    def make_gates(which, role):
        placed, weight = places(which, role, True)
        gates = jnp.transpose(placed * weight)[:TOK]
        high = gates.astype(jnp.bfloat16)
        ghi[which, role] = high
        glo[which, role] = (gates - high.astype(jnp.float32)).astype(jnp.bfloat16)

    def pack(a, role, cols):
        which = 0 if a < F else 1
        sb[a, role * SLOTS : (role + 1) * SLOTS, pl.ds(*cols)] = jnp.dot(
            pt[which, role][:, :TOK], ag[a, role, :, pl.ds(*cols)], preferred_element_type=jnp.float32
        ).astype(jnp.bfloat16)

    def spread(src, dst, role, cols, ssem, rsem):
        def rows(k):
            return pl.ds(pl.multiple_of((role * 8 + k) * MOST, MOST), MOST)

        for dy in (2, 1, 3):
            for core in (0, 1):
                remote(
                    src.at[rows(dy * 2 + core), pl.ds(*cols)],
                    dst.at[rows((4 - dy) * 2 + c), pl.ds(*cols)],
                    ssem,
                    rsem,
                    at(dy, 0, core),
                )
        remote(src.at[rows(1 - c), pl.ds(*cols)], dst.at[rows(c), pl.ds(*cols)], ssem, rsem, at(0, 0, 1 - c))
        pltpu.make_async_copy(src.at[rows(c), pl.ds(*cols)], dst.at[rows(c), pl.ds(*cols)], rsem).start()

    def dispatch(a, role, cols):
        spread(sb.at[a], rx.at[a], role, cols, y_s.at[a], rx_r.at[a])

    def give_back(o, role, cols, part):
        spread(ob.at[o], rt.at[o], role, cols, ret_s.at[o], rt_r.at[o, role, part])

    near, other = at(0, 1, c), at(0, -1, c)

    def half(ref, h):
        return ref.at[:, pl.ds(h * HALF, HALF)]

    def send_c(h):
        for role in (0, 1):
            remote(
                half(bwd_ref, h), half(ag.at[C, role], h), seg_s.at[2 * h + role], ag_r.at[C, role, h], at(0, role, c, -1)
            )

    pl.semaphore_wait(barrier, len(partners))
    send_c(0)
    for load in loads:
        load.wait()
    meta[0] = jnp.full((16, SLOTS), -1.0, jnp.float32)
    for i, ref in enumerate((b_routes_ref, b_gates_ref, f_routes_ref, f_gates_ref)):
        meta[0, 4 * i : 4 * i + 4, :TOK] = ref[...].astype(jnp.float32)
    for i, role in enumerate((1, 3, 2)):
        remote(meta.at[0], meta.at[4 - role], meta_s.at[i], meta_r.at[4 - role], at(0, role, c))
    send_c(1)
    for role in (0, 1):
        remote(fwd_ref, fraw.at[role], seg_s.at[4 + role], ag_r.at[F, role, 0], at(0, role, c, 1))
    ag[B, 0] = normalized(stored_ref[...])
    make_pack(0, 0)
    pack(B, 0, FULL)
    dispatch(B, 0, FULL)
    for i, (role, h) in enumerate(((1, 0), (3, 1), (1, 1), (3, 0))):
        dest = near if role == 1 else other
        remote(half(ag.at[B, 0], h), half(ag.at[B, 4 - role], h), ag_s.at[B, i], ag_r.at[B, 4 - role, h], dest)


    def hop_b(role, h):
        wait(half(ag.at[B, role], h), ag_r.at[B, role, h])
        if (role, h) == (3, 0):
            remote(half(ag.at[B, 3], 0), half(ag.at[B, 2], 0), ag_s.at[B, 4], ag_r.at[B, 2, 0], near)
        if (role, h) == (1, 1):
            remote(half(ag.at[B, 1], 1), half(ag.at[B, 2], 1), ag_s.at[B, 5], ag_r.at[B, 2, 1], other)
        pack(B, role, (h * HALF, HALF))
        dispatch(B, role, (h * HALF, HALF))

    def hop_c(role, h):
        wait(half(ag.at[C, role], h), ag_r.at[C, role, h])
        pack(C, role, (h * HALF, HALF))
        dispatch(C, role, (h * HALF, HALF))

    def hop_f(role):
        wait(fraw.at[role], ag_r.at[F, role, 0])
        if role == 0:
            remote(fraw.at[0], fraw.at[3], ag_s.at[F, 0], ag_r.at[F, 3, 0], near)
        if role == 1:
            remote(fraw.at[1], fraw.at[2], ag_s.at[F, 1], ag_r.at[F, 2, 0], other)
        ag[F, role] = normalized(fraw[role])
        pack(F, role, FULL)
        dispatch(F, role, FULL)

    hop_c(0, 0)
    for role in (1, 3, 2):
        wait(meta.at[role], meta_r.at[role])
        make_pack(0, role)
    hop_c(1, 0)
    hop_c(0, 1)
    hop_c(1, 1)
    make_pack(1, 0)
    make_pack(1, 1)
    hop_f(0)
    hop_f(1)
    for h in (0, 1):
        remote(half(ag.at[C, 0], h), half(ag.at[C, 3], h), ag_s.at[C, h], ag_r.at[C, 3, h], near)
        remote(half(ag.at[C, 1], h), half(ag.at[C, 2], h), ag_s.at[C, 2 + h], ag_r.at[C, 2, h], other)
    hop_b(3, 0)
    hop_b(1, 1)
    hop_b(3, 1)
    hop_b(1, 0)
    make_pack(1, 3)
    make_pack(1, 2)
    for role in range(4):
        make_gates(1, role)
        make_gates(0, role)
    hop_f(3)
    hop_f(2)
    hop_c(3, 0)
    hop_c(2, 0)
    hop_c(3, 1)
    hop_c(2, 1)
    hop_b(2, 0)
    hop_b(2, 1)


    def tile(n):
        return pl.ds(pl.multiple_of(n * TILE, TILE), TILE)

    nt = (((1,), (1,)), ((), ()))

    def back_in(n, carry):
        pre = jnp.dot(rx[B], up[:, tile(n)], preferred_element_type=jnp.float32)
        sigma = jax.nn.sigmoid(pre)
        deriv = sigma * (1.0 + pre * (1.0 - sigma))
        back = lax.dot_general(rx[C], down[tile(n), :], nt, preferred_element_type=jnp.float32)
        mid[:, tile(n)] = (back * deriv).astype(jnp.bfloat16)
        return carry

    def back_out(n, carry):
        ob[OB_, :, tile(n)] = lax.dot_general(
            mid[...], up[tile(n), :], nt, preferred_element_type=jnp.float32
        ).astype(jnp.bfloat16)
        return carry

    def front_in(n, carry):
        pre = jnp.dot(rx[F], up[:, tile(n)], preferred_element_type=jnp.float32)
        mid[:, tile(n)] = jax.nn.silu(pre).astype(jnp.bfloat16)
        return carry

    def front_out(n, carry):
        ob[OF_, :, tile(n)] = jnp.dot(mid[...], down[:, tile(n)], preferred_element_type=jnp.float32).astype(
            jnp.bfloat16
        )
        return carry

    def gather(o, role, h):
        lane = pl.ds(h * HALF, HALF)
        block = rt.at[o, pl.ds(role * SLOTS, SLOTS), lane]
        wait(block, rt_r.at[o, role, h])
        rows = block[...]
        total = jnp.dot(ghi[o, role], rows, preferred_element_type=jnp.float32) + jnp.dot(
            glo[o, role], rows, preferred_element_type=jnp.float32
        )
        if role == 0:
            acc[o, :, lane] = total
            return
        if (role, h) in ((1, 0), (3, 1)):
            wait(half(fr.at[o], h), fr_r.at[o, h])
            total += fr[o, :, lane].astype(jnp.float32)
        ps[o, role, :, lane] = total.astype(jnp.bfloat16)
        if role == 2:
            remote(half(ps.at[o, 2], h), half(fr.at[o], h), fr_s.at[o, h], fr_r.at[o, h], near if h == 0 else other)
        else:
            i = 0 if role == 1 else 1
            remote(
                half(ps.at[o, role], h),
                half(hs.at[o, i], h),
                hs_s.at[o, i, h],
                hs_r.at[o, i, h],
                near if role == 1 else other,
            )

    def summed(o, h):
        lane = pl.ds(h * HALF, HALF)
        for i in (0, 1):
            wait(half(hs.at[o, i], h), hs_r.at[o, i, h])
        return acc[o, :, lane] + hs[o, 0, :, lane].astype(jnp.float32) + hs[o, 1, :, lane].astype(jnp.float32)

    def give_back_sides(o):
        for part, cols in enumerate((H0, H1)):
            give_back(o, 1, cols, part)
            give_back(o, 3, cols, part)

    up_copy.wait()
    down_copy.wait()
    wait(rx.at[F], rx_r.at[F])
    lax.fori_loop(0, 6, front_in, 0)
    lax.fori_loop(0, 6, front_out, 0)
    give_back(OF_, 2, H0, 0)
    give_back(OF_, 2, H1, 1)
    give_back_sides(OF_)

    wait(rx.at[B], rx_r.at[B])
    wait(rx.at[C], rx_r.at[C])
    lax.fori_loop(0, 3, back_in, 0)
    gather(OF_, 2, 0)
    gather(OF_, 2, 1)
    lax.fori_loop(3, 6, back_in, 0)
    gather(OF_, 1, 0)
    gather(OF_, 3, 0)
    lax.fori_loop(0, 3, back_out, 0)
    give_back(OB_, 2, H0, 0)
    lax.fori_loop(3, 6, back_out, 0)
    give_back(OB_, 2, H1, 1)
    gather(OF_, 1, 1)
    gather(OF_, 3, 1)
    give_back_sides(OB_)
    gather(OB_, 2, 0)
    gather(OB_, 2, 1)
    for o in (OB_, OF_):
        for part, cols in enumerate((H0, H1)):
            give_back(o, 0, cols, part)
    gather(OB_, 1, 0)
    gather(OB_, 3, 0)
    gather(OB_, 1, 1)
    gather(OB_, 3, 1)
    gather(OB_, 0, 0)
    gather(OB_, 0, 1)
    for h in (0, 1):
        acc[OB_, :, pl.ds(h * HALF, HALF)] = summed(OB_, h)
    weighted = gain_ref[...] * acc[OB_]
    values = stored_ref[...].astype(jnp.float32)
    scale = scale_of(values)
    correction = values * (scale * scale * scale) * jnp.mean(values * weighted, axis=-1, keepdims=True)
    bout_ref[...] = (ag[C, 0].astype(jnp.float32) + scale * weighted - correction).astype(jnp.bfloat16)

    for h in (0, 1):
        gather(OF_, 0, h)
        lane = pl.ds(h * HALF, HALF)
        fout_ref[:, lane] = (fraw[0, :, lane].astype(jnp.float32) + summed(OF_, h)).astype(jnp.bfloat16)

    for i in range(3):
        wait(meta.at[0], meta_s.at[i])
    for i in range(4):
        wait(half(ag.at[C, 0], 0), seg_s.at[i])
        wait(half(ag.at[C, 0], 0), ag_s.at[C, i])
    for i in range(6):
        wait(half(ag.at[B, 0], 0), ag_s.at[B, i])
    for i in range(2):
        wait(fraw.at[0], seg_s.at[4 + i])
        wait(fraw.at[0], ag_s.at[F, i])
    sent = pl.ds(0, ROWS * 7 // 8)
    for a in (B, C, F):
        wait(sb.at[a, sent], y_s.at[a])
    for o in (OB_, OF_):
        wait(ob.at[o, sent], ret_s.at[o])
        for h in (0, 1):
            wait(half(fr.at[o], h), fr_s.at[o, h])
            for i in (0, 1):
                wait(half(hs.at[o, i], h), hs_s.at[o, i, h])


def finish(fwd_ref, bwd_ref, fout_ref, bout_ref, sem):
    first = pltpu.make_async_copy(fwd_ref, fout_ref, sem.at[0])
    second = pltpu.make_async_copy(bwd_ref, bout_ref, sem.at[1])
    first.start()
    second.start()
    first.wait()
    second.wait()


def section(fwd_prev, bwd_prev, stored_in, fwd_routes, fwd_gates, bwd_routes, bwd_gates, norm_gain, w_up, w_down):
    vmem = pl.BlockSpec(memory_space=pltpu.VMEM)
    anywhere = pl.BlockSpec(memory_space=pl.ANY)
    bf16, f32 = jnp.bfloat16, jnp.float32
    dma = pltpu.SemaphoreType.DMA
    out = jax.ShapeDtypeStruct((TOK, D), bf16)
    kept = pltpu.VMEM((TOK, D), bf16)
    fwd_out, bwd_out = pl.pallas_call(
        kernel,
        out_shape=(kept, kept),
        in_specs=[anywhere] * 10,
        out_specs=(vmem, vmem),
        scratch_shapes=[
            pltpu.VMEM((D, D), bf16),
            pltpu.VMEM((D, D), bf16),
            pltpu.VMEM((TOK, D), bf16),
            pltpu.VMEM((4, TOK), jnp.int32),
            pltpu.VMEM((4, TOK), f32),
            pltpu.VMEM((4, TOK), jnp.int32),
            pltpu.VMEM((4, TOK), f32),
            pltpu.VMEM((1, D), f32),
            pltpu.VMEM((4, 16, SLOTS), f32),
            pltpu.VMEM((3, 4, TOK, D), bf16),
            pltpu.VMEM((4, TOK, D), bf16),
            pltpu.VMEM((3, ROWS, D), bf16),
            pltpu.VMEM((3, ROWS, D), bf16),
            pltpu.VMEM((ROWS, D), bf16),
            pltpu.VMEM((2, ROWS, D), bf16),
            pltpu.VMEM((2, ROWS, D), bf16),
            pltpu.VMEM((2, 4, TOK, D), bf16),
            pltpu.VMEM((2, TOK, D), bf16),
            pltpu.VMEM((2, 2, TOK, D), bf16),
            pltpu.VMEM((2, TOK, D), f32),
            pltpu.VMEM((2, 4, SLOTS, SLOTS), bf16),
            pltpu.VMEM((2, 4, TOK, SLOTS), bf16),
            pltpu.VMEM((2, 4, TOK, SLOTS), bf16),
            dma((6,)),
            dma((2,)),
            dma((3,)),
            dma((4,)),
            dma((6,)),
            dma((3, 6)),
            dma((3, 4, 2)),
            dma((3,)),
            dma((3,)),
            dma((2,)),
            dma((2, 4, 2)),
            dma((2, 2)),
            dma((2, 2)),
            dma((2, 2, 2)),
            dma((2, 2, 2)),
        ],
        compiler_params=pltpu.CompilerParams(collective_id=0, has_side_effects=True, vmem_limit_bytes=56 * 2**20),
        cost_estimate=pl.CostEstimate(
            flops=5 * 2 * ROWS * D * D, bytes_accessed=2 * D * D * 2 + 5 * TOK * D * 2, transcendentals=2 * ROWS * D
        ),
        name="section",
    )(
        fwd_prev[0],
        bwd_prev[0],
        stored_in[0],
        bwd_routes[0].T,
        bwd_gates[0].T,
        fwd_routes[0].T,
        fwd_gates[0].T,
        norm_gain,
        w_up[0, 0],
        w_down[0, 0],
    )
    fwd_out, bwd_out = pl.pallas_call(
        finish,
        out_shape=(out, out),
        in_specs=[vmem] * 2,
        out_specs=(anywhere, anywhere),
        scratch_shapes=[dma((2,))],
        name="finish",
    )(*(pltpu.with_memory_space_constraint(v, pltpu.VMEM) for v in (fwd_out, bwd_out)))
    return fwd_out[None], bwd_out[None]


def solution(mesh):
    block = P("segment", "expert", None)
    weight = P("segment", "expert", None, None)
    return jax.shard_map(
        section,
        mesh=mesh,
        in_specs=(block,) * 7 + (P("segment", None), weight, weight),
        out_specs=(block, block),
        check_vma=False,
    )
```

```python
import functools

import jax
import jax.numpy as jnp
from jax import lax
from jax.experimental import pallas as pl
from jax.experimental.pallas import tpu as pltpu
from jax.sharding import PartitionSpec as P

MESH = pl.DeviceIdType.MESH
TOK = 64
D = 1536
MOST = 16
SLOTS = 128
ROWS = 512
HALF = D // 2
TILE = 256
EPS = 1e-05

B, C, F = 0, 1, 2
OB_, OF_ = 0, 1
H0, H1 = (0, HALF), (HALF, HALF)
FULL = (0, D)


def kernel(
    fwd_ref,
    bwd_ref,
    stored_hbm,
    b_routes_hbm,
    b_gates_hbm,
    f_routes_hbm,
    f_gates_hbm,
    gain_hbm,
    up_hbm,
    down_hbm,
    fout_ref,
    bout_ref,
    up,
    down,
    stored_ref,
    b_routes_ref,
    b_gates_ref,
    f_routes_ref,
    f_gates_ref,
    gain_ref,
    meta,
    ag,
    fraw,
    sb,
    rx,
    mid,
    ob,
    rt,
    ps,
    fr,
    hs,
    acc,
    pt,
    ghi,
    glo,
    load_sem,
    wsem,
    meta_s,
    meta_r,
    seg_s,
    ag_s,
    ag_r,
    y_s,
    rx_r,
    ret_s,
    rt_r,
    fr_s,
    fr_r,
    hs_s,
    hs_r,
):
    s = lax.axis_index("segment")
    e = lax.axis_index("expert")
    y, z, c = e // 8, (e // 2) % 4, e % 2
    g = 2 * (s % 2) - 1

    def at(dy, role, core, ds=0):
        return (
            (s + ds + 8) % 8,
            ((y + dy) % 4) * 8 + ((z + role * g + 4) % 4) * 2 + core,
        )

    def remote(src, dst, ssem, rsem, device):
        copy = pltpu.make_async_remote_copy(
            src_ref=src, dst_ref=dst, send_sem=ssem, recv_sem=rsem, device_id=device, device_id_type=MESH
        )
        copy.start()

    def wait(ref, sem):
        pltpu.make_async_copy(ref, ref, sem).wait()

    partners = [at(dy, 0, core) for dy in (1, 2, 3) for core in (0, 1)]
    partners += [at(0, 0, 1 - c), at(0, 1, c), at(0, -1, c), at(0, 2, c)]
    partners += [at(0, 0, c, 1), at(0, 1, c, 1), at(0, 0, c, -1), at(0, 1, c, -1)]
    barrier = pltpu.get_barrier_semaphore()
    for device in partners:
        pl.semaphore_signal(barrier, inc=1, device_id=device, device_id_type=MESH)

    loads = [
        pltpu.make_async_copy(src, dst, load_sem.at[i])
        for i, (src, dst) in enumerate(
            (
                (stored_hbm, stored_ref),
                (b_routes_hbm, b_routes_ref),
                (b_gates_hbm, b_gates_ref),
                (f_routes_hbm, f_routes_ref),
                (f_gates_hbm, f_gates_ref),
                (gain_hbm, gain_ref),
            )
        )
    ]
    for load in loads:
        load.start()
    up_copy = pltpu.make_async_copy(up_hbm, up, wsem.at[0])
    down_copy = pltpu.make_async_copy(down_hbm, down, wsem.at[1])
    up_copy.start()
    down_copy.start()

    def scale_of(values):
        return lax.rsqrt(jnp.mean(values * values, axis=-1, keepdims=True) + EPS)

    def normalized(rows):
        values = rows.astype(jnp.float32)
        return (values * scale_of(values) * gain_ref[...]).astype(jnp.bfloat16)

    slot = lax.broadcasted_iota(jnp.int32, (SLOTS, SLOTS), 0)
    group = slot // MOST
    expert_of = (((y + group // 2) % 4) * 8 + z * 2 + group % 2).astype(jnp.float32)
    rank_of = (slot % MOST).astype(jnp.float32)
    before = (slot < lax.broadcasted_iota(jnp.int32, (SLOTS, SLOTS), 1)).astype(jnp.bfloat16)

    def places(which, role, gates):
        base = 8 * which
        chosen = jnp.zeros((SLOTS, SLOTS), jnp.float32)
        weight = jnp.zeros((SLOTS, SLOTS), jnp.float32)
        for k in range(4):
            same = (meta[role, base + k : base + k + 1, :] == expert_of).astype(jnp.float32)
            chosen += same
            if gates:
                weight += same * meta[role, base + 4 + k : base + 5 + k, :]
        rank = jnp.dot(chosen.astype(jnp.bfloat16), before, preferred_element_type=jnp.float32)
        placed = chosen * (rank == rank_of).astype(jnp.float32)
        return placed, weight

    def make_pack(which, role):
        placed, _ = places(which, role, False)
        pt[which, role] = placed.astype(jnp.bfloat16)

    def make_gates(which, role):
        placed, weight = places(which, role, True)
        gates = jnp.transpose(placed * weight)[:TOK]
        high = gates.astype(jnp.bfloat16)
        ghi[which, role] = high
        glo[which, role] = (gates - high.astype(jnp.float32)).astype(jnp.bfloat16)

    def pack(a, role, cols):
        which = 0 if a < F else 1
        sb[a, role * SLOTS : (role + 1) * SLOTS, pl.ds(*cols)] = jnp.dot(
            pt[which, role][:, :TOK], ag[a, role, :, pl.ds(*cols)], preferred_element_type=jnp.float32
        ).astype(jnp.bfloat16)

    def spread(src, dst, role, cols, ssem, rsem):
        def rows(k):
            return pl.ds(pl.multiple_of((role * 8 + k) * MOST, MOST), MOST)

        for dy in (2, 1, 3):
            for core in (0, 1):
                remote(
                    src.at[rows(dy * 2 + core), pl.ds(*cols)],
                    dst.at[rows((4 - dy) * 2 + c), pl.ds(*cols)],
                    ssem,
                    rsem,
                    at(dy, 0, core),
                )
        remote(src.at[rows(1 - c), pl.ds(*cols)], dst.at[rows(c), pl.ds(*cols)], ssem, rsem, at(0, 0, 1 - c))
        pltpu.make_async_copy(src.at[rows(c), pl.ds(*cols)], dst.at[rows(c), pl.ds(*cols)], rsem).start()

    def dispatch(a, role, cols):
        spread(sb.at[a], rx.at[a], role, cols, y_s.at[a], rx_r.at[a])

    def give_back(o, role, cols, part):
        spread(ob.at[o], rt.at[o], role, cols, ret_s.at[o], rt_r.at[o, role, part])

    near, other = at(0, 1, c), at(0, -1, c)

    def half(ref, h):
        return ref.at[:, pl.ds(h * HALF, HALF)]

    def send_c(h):
        for role in (0, 1):
            remote(
                half(bwd_ref, h), half(ag.at[C, role], h), seg_s.at[2 * h + role], ag_r.at[C, role, h], at(0, role, c, -1)
            )

    pl.semaphore_wait(barrier, len(partners))
    send_c(0)
    for load in loads:
        load.wait()
    meta[0] = jnp.full((16, SLOTS), -1.0, jnp.float32)
    for i, ref in enumerate((b_routes_ref, b_gates_ref, f_routes_ref, f_gates_ref)):
        meta[0, 4 * i : 4 * i + 4, :TOK] = ref[...].astype(jnp.float32)
    for i, role in enumerate((1, 3, 2)):
        remote(meta.at[0], meta.at[4 - role], meta_s.at[i], meta_r.at[4 - role], at(0, role, c))
    send_c(1)
    for role in (0, 1):
        remote(fwd_ref, fraw.at[role], seg_s.at[4 + role], ag_r.at[F, role, 0], at(0, role, c, 1))
    ag[B, 0] = normalized(stored_ref[...])
    make_pack(0, 0)
    pack(B, 0, FULL)
    dispatch(B, 0, FULL)
    for i, (role, h) in enumerate(((1, 0), (3, 1), (1, 1), (3, 0))):
        dest = near if role == 1 else other
        remote(half(ag.at[B, 0], h), half(ag.at[B, 4 - role], h), ag_s.at[B, i], ag_r.at[B, 4 - role, h], dest)


    def hop_b(role, h):
        wait(half(ag.at[B, role], h), ag_r.at[B, role, h])
        if (role, h) == (3, 0):
            remote(half(ag.at[B, 3], 0), half(ag.at[B, 2], 0), ag_s.at[B, 4], ag_r.at[B, 2, 0], near)
        if (role, h) == (1, 1):
            remote(half(ag.at[B, 1], 1), half(ag.at[B, 2], 1), ag_s.at[B, 5], ag_r.at[B, 2, 1], other)
        pack(B, role, (h * HALF, HALF))
        dispatch(B, role, (h * HALF, HALF))

    def hop_c(role, h):
        wait(half(ag.at[C, role], h), ag_r.at[C, role, h])
        pack(C, role, (h * HALF, HALF))
        dispatch(C, role, (h * HALF, HALF))

    def hop_f(role):
        wait(fraw.at[role], ag_r.at[F, role, 0])
        if role == 0:
            remote(fraw.at[0], fraw.at[3], ag_s.at[F, 0], ag_r.at[F, 3, 0], near)
        if role == 1:
            remote(fraw.at[1], fraw.at[2], ag_s.at[F, 1], ag_r.at[F, 2, 0], other)
        ag[F, role] = normalized(fraw[role])
        pack(F, role, FULL)
        dispatch(F, role, FULL)

    hop_c(0, 0)
    wait(meta.at[1], meta_r.at[1])
    make_pack(0, 1)
    hop_c(1, 0)
    hop_c(0, 1)
    hop_c(1, 1)
    make_pack(1, 0)
    make_pack(1, 1)
    hop_f(0)
    hop_f(1)
    for h in (0, 1):
        remote(half(ag.at[C, 0], h), half(ag.at[C, 3], h), ag_s.at[C, h], ag_r.at[C, 3, h], near)
        remote(half(ag.at[C, 1], h), half(ag.at[C, 2], h), ag_s.at[C, 2 + h], ag_r.at[C, 2, h], other)
    wait(meta.at[3], meta_r.at[3])
    make_pack(0, 3)
    hop_b(3, 0)
    hop_b(1, 1)
    hop_b(3, 1)
    hop_b(1, 0)
    wait(meta.at[2], meta_r.at[2])
    make_pack(0, 2)
    make_pack(1, 3)
    make_pack(1, 2)
    for role in range(4):
        make_gates(1, role)
        make_gates(0, role)
    hop_f(3)
    hop_f(2)
    hop_c(3, 0)
    hop_c(2, 0)
    hop_c(3, 1)
    hop_c(2, 1)
    hop_b(2, 0)
    hop_b(2, 1)


    def tile(n):
        return pl.ds(pl.multiple_of(n * TILE, TILE), TILE)

    nt = (((1,), (1,)), ((), ()))

    def back_in(n, carry):
        pre = jnp.dot(rx[B], up[:, tile(n)], preferred_element_type=jnp.float32)
        sigma = jax.nn.sigmoid(pre)
        deriv = sigma * (1.0 + pre * (1.0 - sigma))
        back = lax.dot_general(rx[C], down[tile(n), :], nt, preferred_element_type=jnp.float32)
        mid[:, tile(n)] = (back * deriv).astype(jnp.bfloat16)
        return carry

    def back_out(n, carry):
        ob[OB_, :, tile(n)] = lax.dot_general(
            mid[...], up[tile(n), :], nt, preferred_element_type=jnp.float32
        ).astype(jnp.bfloat16)
        return carry

    def front_in(n, carry):
        pre = jnp.dot(rx[F], up[:, tile(n)], preferred_element_type=jnp.float32)
        mid[:, tile(n)] = jax.nn.silu(pre).astype(jnp.bfloat16)
        return carry

    def front_out(n, carry):
        ob[OF_, :, tile(n)] = jnp.dot(mid[...], down[:, tile(n)], preferred_element_type=jnp.float32).astype(
            jnp.bfloat16
        )
        return carry

    def gather(o, role, h):
        lane = pl.ds(h * HALF, HALF)
        block = rt.at[o, pl.ds(role * SLOTS, SLOTS), lane]
        wait(block, rt_r.at[o, role, h])
        rows = block[...]
        total = jnp.dot(ghi[o, role], rows, preferred_element_type=jnp.float32) + jnp.dot(
            glo[o, role], rows, preferred_element_type=jnp.float32
        )
        if role == 0:
            acc[o, :, lane] = total
            return
        if (role, h) in ((1, 0), (3, 1)):
            wait(half(fr.at[o], h), fr_r.at[o, h])
            total += fr[o, :, lane].astype(jnp.float32)
        ps[o, role, :, lane] = total.astype(jnp.bfloat16)
        if role == 2:
            remote(half(ps.at[o, 2], h), half(fr.at[o], h), fr_s.at[o, h], fr_r.at[o, h], near if h == 0 else other)
        else:
            i = 0 if role == 1 else 1
            remote(
                half(ps.at[o, role], h),
                half(hs.at[o, i], h),
                hs_s.at[o, i, h],
                hs_r.at[o, i, h],
                near if role == 1 else other,
            )

    def summed(o, h):
        lane = pl.ds(h * HALF, HALF)
        for i in (0, 1):
            wait(half(hs.at[o, i], h), hs_r.at[o, i, h])
        return acc[o, :, lane] + hs[o, 0, :, lane].astype(jnp.float32) + hs[o, 1, :, lane].astype(jnp.float32)

    def give_back_sides(o):
        for part, cols in enumerate((H0, H1)):
            give_back(o, 1, cols, part)
            give_back(o, 3, cols, part)

    up_copy.wait()
    down_copy.wait()
    wait(rx.at[F], rx_r.at[F])
    lax.fori_loop(0, 6, front_in, 0)
    lax.fori_loop(0, 6, front_out, 0)
    give_back(OF_, 2, H0, 0)
    give_back(OF_, 2, H1, 1)
    give_back_sides(OF_)

    wait(rx.at[B], rx_r.at[B])
    wait(rx.at[C], rx_r.at[C])
    lax.fori_loop(0, 3, back_in, 0)
    gather(OF_, 2, 0)
    gather(OF_, 2, 1)
    lax.fori_loop(3, 6, back_in, 0)
    gather(OF_, 1, 0)
    gather(OF_, 3, 0)
    lax.fori_loop(0, 3, back_out, 0)
    give_back(OB_, 2, H0, 0)
    lax.fori_loop(3, 6, back_out, 0)
    give_back(OB_, 2, H1, 1)
    gather(OF_, 1, 1)
    gather(OF_, 3, 1)
    give_back_sides(OB_)
    gather(OB_, 2, 0)
    gather(OB_, 2, 1)
    for o in (OB_, OF_):
        for part, cols in enumerate((H0, H1)):
            give_back(o, 0, cols, part)
    gather(OB_, 1, 0)
    gather(OB_, 3, 0)
    gather(OB_, 1, 1)
    gather(OB_, 3, 1)
    gather(OB_, 0, 0)
    gather(OB_, 0, 1)
    for h in (0, 1):
        acc[OB_, :, pl.ds(h * HALF, HALF)] = summed(OB_, h)
    weighted = gain_ref[...] * acc[OB_]
    values = stored_ref[...].astype(jnp.float32)
    scale = scale_of(values)
    correction = values * (scale * scale * scale) * jnp.mean(values * weighted, axis=-1, keepdims=True)
    bout_ref[...] = (ag[C, 0].astype(jnp.float32) + scale * weighted - correction).astype(jnp.bfloat16)

    for h in (0, 1):
        gather(OF_, 0, h)
        lane = pl.ds(h * HALF, HALF)
        fout_ref[:, lane] = (fraw[0, :, lane].astype(jnp.float32) + summed(OF_, h)).astype(jnp.bfloat16)

    for i in range(3):
        wait(meta.at[0], meta_s.at[i])
    for i in range(4):
        wait(half(ag.at[C, 0], 0), seg_s.at[i])
        wait(half(ag.at[C, 0], 0), ag_s.at[C, i])
    for i in range(6):
        wait(half(ag.at[B, 0], 0), ag_s.at[B, i])
    for i in range(2):
        wait(fraw.at[0], seg_s.at[4 + i])
        wait(fraw.at[0], ag_s.at[F, i])
    sent = pl.ds(0, ROWS * 7 // 8)
    for a in (B, C, F):
        wait(sb.at[a, sent], y_s.at[a])
    for o in (OB_, OF_):
        wait(ob.at[o, sent], ret_s.at[o])
        for h in (0, 1):
            wait(half(fr.at[o], h), fr_s.at[o, h])
            for i in (0, 1):
                wait(half(hs.at[o, i], h), hs_s.at[o, i, h])


def finish(fwd_ref, bwd_ref, fout_ref, bout_ref, sem):
    first = pltpu.make_async_copy(fwd_ref, fout_ref, sem.at[0])
    second = pltpu.make_async_copy(bwd_ref, bout_ref, sem.at[1])
    first.start()
    second.start()
    first.wait()
    second.wait()


def section(fwd_prev, bwd_prev, stored_in, fwd_routes, fwd_gates, bwd_routes, bwd_gates, norm_gain, w_up, w_down):
    vmem = pl.BlockSpec(memory_space=pltpu.VMEM)
    anywhere = pl.BlockSpec(memory_space=pl.ANY)
    bf16, f32 = jnp.bfloat16, jnp.float32
    dma = pltpu.SemaphoreType.DMA
    out = jax.ShapeDtypeStruct((TOK, D), bf16)
    kept = pltpu.VMEM((TOK, D), bf16)
    fwd_out, bwd_out = pl.pallas_call(
        kernel,
        out_shape=(kept, kept),
        in_specs=[anywhere] * 10,
        out_specs=(vmem, vmem),
        scratch_shapes=[
            pltpu.VMEM((D, D), bf16),
            pltpu.VMEM((D, D), bf16),
            pltpu.VMEM((TOK, D), bf16),
            pltpu.VMEM((4, TOK), jnp.int32),
            pltpu.VMEM((4, TOK), f32),
            pltpu.VMEM((4, TOK), jnp.int32),
            pltpu.VMEM((4, TOK), f32),
            pltpu.VMEM((1, D), f32),
            pltpu.VMEM((4, 16, SLOTS), f32),
            pltpu.VMEM((3, 4, TOK, D), bf16),
            pltpu.VMEM((4, TOK, D), bf16),
            pltpu.VMEM((3, ROWS, D), bf16),
            pltpu.VMEM((3, ROWS, D), bf16),
            pltpu.VMEM((ROWS, D), bf16),
            pltpu.VMEM((2, ROWS, D), bf16),
            pltpu.VMEM((2, ROWS, D), bf16),
            pltpu.VMEM((2, 4, TOK, D), bf16),
            pltpu.VMEM((2, TOK, D), bf16),
            pltpu.VMEM((2, 2, TOK, D), bf16),
            pltpu.VMEM((2, TOK, D), f32),
            pltpu.VMEM((2, 4, SLOTS, SLOTS), bf16),
            pltpu.VMEM((2, 4, TOK, SLOTS), bf16),
            pltpu.VMEM((2, 4, TOK, SLOTS), bf16),
            dma((6,)),
            dma((2,)),
            dma((3,)),
            dma((4,)),
            dma((6,)),
            dma((3, 6)),
            dma((3, 4, 2)),
            dma((3,)),
            dma((3,)),
            dma((2,)),
            dma((2, 4, 2)),
            dma((2, 2)),
            dma((2, 2)),
            dma((2, 2, 2)),
            dma((2, 2, 2)),
        ],
        compiler_params=pltpu.CompilerParams(collective_id=0, has_side_effects=True, vmem_limit_bytes=56 * 2**20),
        cost_estimate=pl.CostEstimate(
            flops=5 * 2 * ROWS * D * D, bytes_accessed=2 * D * D * 2 + 5 * TOK * D * 2, transcendentals=2 * ROWS * D
        ),
        name="section",
    )(
        fwd_prev[0],
        bwd_prev[0],
        stored_in[0],
        bwd_routes[0].T,
        bwd_gates[0].T,
        fwd_routes[0].T,
        fwd_gates[0].T,
        norm_gain,
        w_up[0, 0],
        w_down[0, 0],
    )
    fwd_out, bwd_out = pl.pallas_call(
        finish,
        out_shape=(out, out),
        in_specs=[vmem] * 2,
        out_specs=(anywhere, anywhere),
        scratch_shapes=[dma((2,))],
        name="finish",
    )(*(pltpu.with_memory_space_constraint(v, pltpu.VMEM) for v in (fwd_out, bwd_out)))
    return fwd_out[None], bwd_out[None]


def solution(mesh):
    block = P("segment", "expert", None)
    weight = P("segment", "expert", None, None)
    return jax.shard_map(
        section,
        mesh=mesh,
        in_specs=(block,) * 7 + (P("segment", None), weight, weight),
        out_specs=(block, block),
        check_vma=False,
    )
```
